256 devices in a mesh: wide: 32 (over x_lo, z, core), narrow: 8 (over x_hi, y).
Axes of the slice: x: 4 (x_hi: 2, x_lo: 2; x = x_hi * 2 + x_lo), y: 4, z: 8, core: 2. Of those that a mesh axis runs over, the one named last changes fastest.
Arguments:
- activations: float32 [1024, 17408], P('wide', 'narrow'), may hold values from -6 to 6
- act_basis: float32 [17408, 17408], P('narrow', 'wide'), may hold values from -0.046875 to 0.046875
- grads: float32 [1024, 5120], P(None, 'wide'), may hold values from -0.3 to 0.3
- grad_basis: float32 [5120, 5120], P('wide', 'narrow'), may hold values from -0.078125 to 0.078125
- seq_ids: int32 [1024], replicated, may hold values from 0 to 3, never falling along the last dimension, each value on 1 to 512 neighbouring positions
Outputs:
- eigenvalues: float32 [17408, 5120], P('wide', 'narrow')
The draws below stay inside these ranges and needn't reach their ends.
Inputs may be any that keep to these rules, and one draw needn't show every extreme that they name: `seq_ids`: never falling along the rows; every sequence has at least one row and at most 512 rows, and one sequence has exactly 512.
All inputs are finite; a program needn't handle non-finite values.
Results may differ from the reference program's by a relative error of at most 0.0003.
Values sent between devices are 32-bit elements; how exact they have to be, the bound alone decides.
No kernel may reach another device: no remote copies, remote signals or barrier semaphores. Data moves between devices by JAX's collectives and lax.ppermute only.
A program may use at most 64 MiB of HBM per device.

```python
import math
import jax
import jax.numpy as jnp
import numpy as np
from jax import lax

D_IN = 17408
D_OUT = 5120
ROWS = 1024
SEQS = 4
SEQ_MOST = 512


def levels(stream_key, extent, split, smallest, high):
    level, own = 1.0, jax.random.fold_in(stream_key, 6)
    for position, blocks in split:
        steps = jnp.exp(jax.random.uniform(jax.random.fold_in(own, position), (blocks,), jnp.float32, smallest / len(split), high / len(split)))
        level = level * jnp.repeat(steps, extent[position] // blocks).reshape([-1 if axis == position else 1 for axis in range(len(extent))])
    return level


def profile(number_of, total, most, slope):
    portions = [(1 << 20) // math.isqrt(standing ** slope) + 1 for standing in range(2, number_of + 1)]
    surplus, given = total - most - (number_of - 1), [1] * (number_of - 1)
    while surplus > 0:
        free = [i for i in range(number_of - 1) if given[i] < most]
        pool, remaining = sum([portions[i] for i in free]), surplus
        for i in free:
            addition = min(most - given[i], max(1, remaining * portions[i] // pool), surplus)
            given[i] = given[i] + addition
            surplus = surplus - addition
    return np.array([most] + given)


def uneven_parts(rng, number_of, total, bound, slope):
    if number_of == 2:
        one = jax.random.randint(rng, (), max(1, total - bound), min(bound, total - 1) + 1)
        return jnp.stack([one, total - one])
    lengths = jnp.asarray(profile(number_of, total, bound, slope), jnp.int32)
    couples = (number_of - 1) // 2
    source_of, sink = lengths[1:1 + 2 * couples:2], lengths[2:2 + 2 * couples:2]
    slack = jnp.minimum(source_of - 1, bound - sink)
    moved = jax.random.randint(jax.random.fold_in(rng, 1), (couples,), 0, 1 << 20) % (slack + 1)
    lengths = lengths.at[1:1 + 2 * couples:2].set(source_of - moved).at[2:2 + 2 * couples:2].set(sink + moved)
    return lengths[jax.random.permutation(jax.random.fold_in(rng, 2), number_of)]


def centred(key, extent, width, limit, pieces=(), kind=jnp.bfloat16):
    array = width * jax.random.normal(key, extent, jnp.float32)
    if pieces:
        array = array * levels(key, extent, pieces, -0.22, 0.18)
    return jnp.clip(array, -limit, limit).astype(kind)


def setup_inputs(seed: int = 0) -> dict:
    arg_keys = jax.random.split(jax.random.key(seed), 6)
    activations = centred(arg_keys[0], (ROWS, D_IN), 1.0, 6.0, ((0, 32), (1, 8)), jnp.float32)
    act_basis = centred(arg_keys[1], (D_IN, D_IN), D_IN ** -0.5, 0.046875, ((0, 8), (1, 32)), jnp.float32)
    grads = centred(arg_keys[2], (ROWS, D_OUT), 0.05, 0.3, ((1, 32),), jnp.float32)
    grad_basis = centred(arg_keys[3], (D_OUT, D_OUT), D_OUT ** -0.5, 0.078125, ((0, 32), (1, 8)), jnp.float32)
    seq_ids = jnp.searchsorted(jnp.cumsum(uneven_parts(arg_keys[4], SEQS, ROWS, SEQ_MOST, 0)), jnp.arange(ROWS), side="right").astype(jnp.int32)
    return dict(activations=activations, act_basis=act_basis, grads=grads, grad_basis=grad_basis, seq_ids=seq_ids)


def reference(activations, act_basis, grads, grad_basis, seq_ids):
    highest = lax.Precision.HIGHEST
    rotated_acts = jnp.dot(activations, act_basis, precision=highest, preferred_element_type=jnp.float32)
    rotated_grads = jnp.dot(grads, grad_basis, precision=highest, preferred_element_type=jnp.float32)

    def accumulate(running, seq_label):
        seq_mask = (seq_ids == seq_label).astype(jnp.float32)[:, None]
        moment = jnp.dot(rotated_acts.T, rotated_grads * seq_mask, precision=highest, preferred_element_type=jnp.float32)
        return running + moment * moment, None

    running = jnp.zeros((rotated_acts.shape[1], rotated_grads.shape[1]), jnp.float32)
    running, unused = lax.scan(accumulate, running, jnp.arange(SEQS, dtype=jnp.int32))
    return running / jnp.float32(SEQS)
```

```python
import jax
import jax.numpy as jnp
from jax import lax
from jax.sharding import Mesh
from jax.sharding import PartitionSpec as P

SEQS = 4
SEQ_MOST = 512
SIZES = {"xl": 2, "z": 8, "c": 2, "xh": 2, "y": 4}
WIDE = ("xl", "z", "c")
NARROW = ("xh", "y")
HIGH = lax.Precision.HIGH


def shifted(value, axis, by=1):
    n = SIZES[axis]
    return lax.ppermute(value, axis, [(i, (i + by) % n) for i in range(n)])


def piece(value, index, rows):
    return lax.dynamic_slice_in_dim(value, index * rows, rows, 0)


def pair(axis, own, other):
    first = lax.axis_index(axis) == 0
    return jnp.concatenate([jnp.where(first, own, other), jnp.where(first, other, own)], 0)


def halves_summed(value, axis):
    rows = value.shape[0] // 2
    me = lax.axis_index(axis)
    return piece(value, me, rows) + shifted(piece(value, 1 - me, rows), axis)


def summed(value, axis):
    n = SIZES[axis]
    rows = value.shape[0] // n
    me = lax.axis_index(axis)
    arrived = [shifted(piece(value, (me + by) % n, rows), axis, by) for by in range(1, n)]
    total = piece(value, me, rows)
    for term in arrived:
        total = total + term
    return total


def dot(a, b):
    return jnp.dot(a, b, precision=HIGH, preferred_element_type=jnp.float32)


def gathered_rows(activations):
    own = pair("xl", activations, shifted(activations, "xl"))
    chunks = [own]
    up = down = own
    for _ in range(3):
        up, down = shifted(up, "z", 1), shifted(down, "z", -1)
        chunks.append(jnp.concatenate([up, down], 0))
    far_up = shifted(up[:32], "z", 1)
    far_down = shifted(down[32:], "z", -1)
    chunks.append(jnp.concatenate([far_up, far_down], 0))
    return chunks


def reduced_chunk(partial):
    cols = partial.shape[1] // 2
    part = halves_summed(summed(partial, "y"), "xh")
    mine = pair("c", part[:, :cols][None], shifted(part[:, cols:], "c")[None])
    both = jnp.stack([mine, shifted(mine, "xh")])
    first = lax.axis_index("xh") == 0
    both = jnp.where(first, both, both[::-1])
    block = jnp.swapaxes(both, 0, 1).reshape(-1, cols)
    return [block] + [shifted(block, "y", by) for by in (1, 2, 3)]


def rotated_activations(activations, own_basis, other_basis):
    rows_in_all = 1024
    chunks = gathered_rows(activations)
    z, y = lax.axis_index("z"), lax.axis_index("y")
    whole = jnp.zeros((rows_in_all, own_basis.shape[1]), jnp.float32)
    for distance, chunk in enumerate(chunks):
        partial = jnp.concatenate([dot(chunk, own_basis), dot(chunk, other_basis)], 1)
        for by, block in enumerate(reduced_chunk(partial)):
            of = (y - by) % 4
            if 0 < distance < 4:
                xl, way = of % 2, of // 2
                at = (z + jnp.where(way == 0, -distance, distance)) % 8
                spot = (xl * 8 + at) * 64
                whole = lax.dynamic_update_slice_in_dim(whole, block, spot, 0)
            else:
                xl, at = of // 2, (z + distance) % 8
                sixteen = (of % 2) * 16
                spot = (xl * 8 + at) * 64 + sixteen
                for core in range(2):
                    whole = lax.dynamic_update_slice_in_dim(
                        whole, block[core * 16 : core * 16 + 16], spot + 32 * core, 0
                    )
    return whole


def rotated_gradients(grads, grad_basis):
    part = dot(grads, grad_basis)
    part = halves_summed(halves_summed(part, "c"), "xl")
    part = summed(part, "z")
    z = lax.axis_index("z")
    rows = part.shape[0]
    whole = jnp.zeros((8 * rows, part.shape[1]), jnp.float32)
    whole = lax.dynamic_update_slice_in_dim(whole, part, z * rows, 0)
    for by in range(1, 8):
        whole = lax.dynamic_update_slice_in_dim(
            whole, shifted(part, "z", by), ((z - by) % 8) * rows, 0
        )
    whole = pair("xl", whole, shifted(whole, "xl"))
    return pair("c", whole, shifted(whole, "c"))


def seq_window(rotated_acts, rotated_grads, seq_ids, seq_label):
    token_rows = rotated_grads.shape[0]
    first_row = jnp.sum((seq_ids < seq_label).astype(jnp.int32))
    window_start = jnp.minimum(first_row, token_rows - SEQ_MOST)
    acts_window = lax.dynamic_slice_in_dim(rotated_acts, window_start, SEQ_MOST, 0)
    grads_window = lax.dynamic_slice_in_dim(rotated_grads, window_start, SEQ_MOST, 0)
    ids_window = lax.dynamic_slice_in_dim(seq_ids, window_start, SEQ_MOST, 0)
    seq_mask = (ids_window == seq_label).astype(jnp.float32)[:, None]
    return (acts_window, grads_window * seq_mask)


def per_device(activations, act_basis, grads, grad_basis, seq_ids):
    rotated_acts = rotated_activations(activations, act_basis, shifted(act_basis, "c"))
    rotated_grads = rotated_gradients(grads, grad_basis)
    running = jnp.zeros((rotated_acts.shape[1], rotated_grads.shape[1]), jnp.float32)
    for seq_label in range(SEQS):
        acts_window, grads_window = seq_window(rotated_acts, rotated_grads, seq_ids, seq_label)
        moment = dot(acts_window.T, grads_window)
        running = running + moment * moment
    return running / jnp.float32(SEQS)


def solution(mesh):
    split = Mesh(mesh.devices.reshape(tuple(SIZES.values())), tuple(SIZES))
    return jax.shard_map(
        per_device,
        mesh=split,
        in_specs=(P(WIDE, NARROW), P(NARROW, WIDE), P(None, WIDE), P(WIDE, NARROW), P()),
        out_specs=P(WIDE, NARROW),
        check_vma=False,
    )
```

```python
import functools

import jax
import jax.numpy as jnp
from jax import lax
from jax.experimental import pallas as pl
from jax.experimental.pallas import tpu as pltpu
from jax.sharding import Mesh
from jax.sharding import PartitionSpec as P

SEQS = 4
SIZES = {"xl": 2, "z": 8, "c": 2, "xh": 2, "y": 4}
WIDE = ("xl", "z", "c")
NARROW = ("xh", "y")
TOKENS = 1024
BLOCK = 32
DEPTH = 256
FIRST, SECOND, LAST = (0, -1, 1), (-2, 2, -3, 3), 4
VMEM = pl.BlockSpec(memory_space=pltpu.VMEM)
SMEM = pl.BlockSpec(memory_space=pltpu.SMEM)
COST = pl.CostEstimate(flops=1000, bytes_accessed=1000, transcendentals=0)


def shifted(value, axis, by=1):
    n = SIZES[axis]
    return lax.ppermute(value, axis, [(i, (i + by) % n) for i in range(n)])


def after(value, other):
    return lax.optimization_barrier((value, other))[0]


def swapped(value, axes):
    return lax.all_to_all(value, axes, 0, 0)


def halved(value):
    high = value.astype(jnp.bfloat16)
    return high, (value - high.astype(jnp.float32)).astype(jnp.bfloat16)


def call(kernel, shapes, in_specs, scratch=(), name=None, mib=12):
    return pl.pallas_call(
        kernel,
        out_shape=shapes,
        in_specs=in_specs,
        out_specs=jax.tree.map(lambda _: VMEM, shapes),
        scratch_shapes=list(scratch),
        compiler_params=pltpu.CompilerParams(vmem_limit_bytes=mib << 20),
        cost_estimate=COST,
        name=name,
    )


def f32(*shape):
    return jax.ShapeDtypeStruct(shape, jnp.float32)


def bf16(*shape):
    return jax.ShapeDtypeStruct(shape, jnp.bfloat16)


def basis_kernel(own, other, high, low):
    rows = own.shape[0]
    for at, ref in enumerate((own, other)):
        into = slice(at * rows, (at + 1) * rows)
        high[into, :], low[into, :] = halved(ref[...])


def split_basis(own, other):
    rows, depth = own.shape
    shape = bf16(2 * rows, depth)
    return call(basis_kernel, [shape, shape], [VMEM, VMEM], name="split_basis")(own, other)


def products_kernel(*refs):
    *blocks, basis_high, basis_low, out, both = refs
    total = out.shape[0]
    at = 0
    for ref in blocks:
        rows = ref.shape[0]
        high, low = halved(ref[...])
        both[at : at + rows, :] = high
        both[total + at : total + at + rows, :] = low
        at += rows

    def product(a, b):
        return lax.dot_general(
            a, b, (((1,), (1,)), ((), ())), preferred_element_type=jnp.float32
        )

    main = product(both[...], basis_high[...])
    out[...] = main[:total] + (main[total:] + product(both[:total, :], basis_low[...]))


def products(blocks, basis):
    rows = sum(block.shape[0] for block in blocks)
    cols, depth = basis[0].shape
    return call(
        products_kernel,
        f32(rows, cols),
        [VMEM] * (len(blocks) + 2),
        [pltpu.VMEM((2 * rows, depth), jnp.bfloat16)],
        name="products",
    )(*blocks, *basis)


def sum_kernel(*refs):
    *arrived, out = refs
    at = 0
    for ref in arrived:
        total = ref[0]
        for k in range(1, ref.shape[0]):
            total = total + ref[k]
        rows = total.shape[0]
        for k in range(out.shape[0]):
            out[k, at : at + rows, :] = total
        at += rows


def sum_copies(*arrived):
    n, _, cols = arrived[0].shape
    rows = sum(part.shape[1] for part in arrived)
    return call(sum_kernel, f32(n, rows, cols), [VMEM] * len(arrived), name="sum_copies")(*arrived)


def in_pieces(value, n):
    return value.reshape(n, -1, value.shape[1])


def grads_kernel(place, grads, basis, own, other):
    rows = own.shape[0]
    basis_high, basis_low = halved(basis[...])

    def product(a, b):
        return lax.dot_general(
            a, b, (((0,), (0,)), ((), ())), preferred_element_type=jnp.float32
        )

    for out, half in ((other, 1 - place[1]), (own, place[1])):
        high, low = halved(grads[:, pl.ds(pl.multiple_of(half * rows, rows), rows)])
        out[...] = product(high, basis_high) + (
            product(low, basis_high) + product(high, basis_low)
        )


def add_kernel(a, b, out):
    out[...] = a[...] + b[...]


def split_store(value, high_ref, low_ref, row):
    high = value.astype(jnp.bfloat16)
    rows = pl.ds(pl.multiple_of(row, BLOCK), value.shape[0])
    high_ref[rows, :] = high
    low_ref[rows, :] = (value - high.astype(jnp.float32)).astype(jnp.bfloat16)


def moments_kernel(place, bounds, *refs):
    acts_refs, grads_refs, out = refs[:4], refs[4:6], refs[6]
    acts_high, acts_low, grads_high, grads_low, moment = refs[7:]
    z, core, lo = place[0], place[1], place[2]
    cols = out.shape[0]
    for from_other in range(2):
        of_core = 1 - core if from_other else core
        first, second = acts_refs[2 * from_other : 2 * from_other + 2]
        sides = slice(cols, 2 * cols) if from_other else slice(0, cols)

        def store(value, distance, far):
            xl = 1 - lo if far else lo
            row = ((xl * 8 + lax.rem(z + distance + 8, 8)) * 2 + of_core) * BLOCK
            split_store(value, acts_high, acts_low, row)

        for at in range(6):
            store(first[at * BLOCK : (at + 1) * BLOCK, sides], FIRST[at // 2], at % 2)
        step = second.shape[0] // 8
        for at in range(8):
            store(second[at * step : at * step + BLOCK, sides], SECOND[at // 2], at % 2)
        for far in range(2):
            ends = [
                second[at * step + BLOCK : (at + 1) * step, sides]
                for at in range(4 * far, 4 * far + 4)
            ]
            store(jnp.concatenate(ends, 0), LAST, far)
        ref = grads_refs[from_other]
        rows = pl.ds(pl.multiple_of(of_core * ref.shape[0], ref.shape[0]), ref.shape[0])
        grads_high[rows, :], grads_low[rows, :] = halved(ref[...])

    def product(a, b):
        return lax.dot_general(
            a, b, (((0,), (0,)), ((), ())), preferred_element_type=jnp.float32
        )

    for seq in range(SEQS):
        first, end = bounds[seq], bounds[seq + 1]
        moment[...] = jnp.zeros_like(moment)

        def block(step, carry):
            rows = pl.ds(pl.multiple_of(step * DEPTH, DEPTH), DEPTH)
            number = step * DEPTH + lax.broadcasted_iota(jnp.int32, (DEPTH, 1), 0)
            mine = (number >= first) & (number < end)
            grads_h = jnp.where(mine, grads_high[rows, :].astype(jnp.float32), 0.0).astype(jnp.bfloat16)
            grads_l = jnp.where(mine, grads_low[rows, :].astype(jnp.float32), 0.0).astype(jnp.bfloat16)
            acts_h, acts_l = acts_high[rows, :], acts_low[rows, :]
            moment[...] += product(acts_h, grads_h) + (
                product(acts_l, grads_h) + product(acts_h, grads_l)
            )
            return carry

        lax.fori_loop(first // DEPTH, (end + DEPTH - 1) // DEPTH, block, 0)
        squared = moment[...] * moment[...]
        if seq == 0:
            out[...] = squared
        elif seq < SEQS - 1:
            out[...] += squared
        else:
            out[...] = (out[...] + squared) * (1.0 / SEQS)


def eigenvalues(place, acts, grads, seq_ids):
    labels = jnp.arange(SEQS + 1, dtype=jnp.int32)
    bounds = jnp.sum((seq_ids[None, :] < labels[:, None]).astype(jnp.int32), axis=1)
    cols, out_cols = acts[0].shape[1] // 2, grads[0].shape[1]
    return call(
        moments_kernel,
        f32(cols, out_cols),
        [SMEM, SMEM] + [VMEM] * (len(acts) + len(grads)),
        [
            pltpu.VMEM((TOKENS, cols), jnp.bfloat16),
            pltpu.VMEM((TOKENS, cols), jnp.bfloat16),
            pltpu.VMEM((TOKENS, out_cols), jnp.bfloat16),
            pltpu.VMEM((TOKENS, out_cols), jnp.bfloat16),
            pltpu.VMEM((cols, out_cols), jnp.float32),
        ],
        name="moments",
        mib=28,
    )(place, bounds, *acts, *grads)


def tied(values, *others):
    held = lax.optimization_barrier((tuple(values), others))
    return list(held[0])


def per_device(activations, act_basis, grads, grad_basis, seq_ids):
    place = jnp.stack([lax.axis_index("z"), lax.axis_index("c"), lax.axis_index("xl")])
    place = place.astype(jnp.int32)
    half, cols = grads.shape[0] // 2, grad_basis.shape[1]

    other_basis = shifted(act_basis, "c").T
    block = jnp.concatenate([activations, shifted(activations, "xl")], 0)
    own, other = call(
        grads_kernel, [f32(half, cols)] * 2, [SMEM, VMEM, VMEM], name="rotate_grads"
    )(place, grads.T, grad_basis)
    block, own, other = tied([block, own, other])

    near = [shifted(block, "z", 1), shifted(block, "z", -1)]
    part = call(add_kernel, f32(half, cols), [VMEM, VMEM], name="add")(own, shifted(other, "c"))
    basis = split_basis(act_basis.T, other_basis)
    part, *basis = tied([part, *basis])
    near = tied(near, part, basis[0])
    part = lax.psum_scatter(part, "z", tiled=True)

    second = [shifted(near[0], "z", 1), shifted(near[1], "z", -1)]
    first_products = products([block, *near], basis)
    *second, first_products = tied([*second, first_products])

    third = [shifted(second[0], "z", 1), shifted(second[1], "z", -1)]
    first_arrived = swapped(in_pieces(first_products, 8), NARROW)
    *third, first_arrived = tied([*third, first_arrived])

    far = [shifted(third[0][:BLOCK], "z", 1), shifted(third[1][BLOCK:], "z", -1)]
    second_products = products([*second, *third], basis)
    first_acts = swapped(sum_copies(first_arrived), NARROW)
    part = part + shifted(part, "xl")
    *far, second_products, part = tied([*far, second_products, part])
    part = lax.all_gather(part, "z", tiled=True)

    third_products = products(far, basis)
    tail = jnp.concatenate([in_pieces(second_products, 8), in_pieces(third_products, 8)], 1)
    tail, first_acts = tied([tail, first_acts])
    second_arrived = swapped(tail, NARROW)
    second_acts = swapped(sum_copies(second_arrived), NARROW)
    acts = [first_acts, second_acts]
    parts = [part, shifted(part, "c")]
    acts = acts + [shifted(value, "c") for value in acts]
    flat = [value.reshape(-1, value.shape[2]) for value in acts]
    return eigenvalues(place, flat, parts, seq_ids)


def solution(mesh):
    split = Mesh(mesh.devices.reshape(tuple(SIZES.values())), tuple(SIZES))
    return jax.shard_map(
        per_device,
        mesh=split,
        in_specs=(P(WIDE, NARROW), P(NARROW, WIDE), P(None, WIDE), P(WIDE, NARROW), P()),
        out_specs=P(WIDE, NARROW),
        check_vma=False,
    )
```

```python
import functools

import jax
import jax.numpy as jnp
from jax import lax
from jax.experimental import pallas as pl
from jax.experimental.pallas import tpu as pltpu
from jax.sharding import Mesh
from jax.sharding import PartitionSpec as P

SEQS = 4
SIZES = {"xl": 2, "z": 8, "c": 2, "xh": 2, "y": 4}
WIDE = ("xl", "z", "c")
NARROW = ("xh", "y")
TOKENS = 1024
BLOCK = 32
DEPTH = 256
TILE = 256
FIRST, SECOND, LAST = (0, -1, 1, -2, 2), (-3, 3), 4
VMEM = pl.BlockSpec(memory_space=pltpu.VMEM)
SMEM = pl.BlockSpec(memory_space=pltpu.SMEM)


def shifted(value, axis, by=1):
    n = SIZES[axis]
    return lax.ppermute(value, axis, [(i, (i + by) % n) for i in range(n)])


def after(value, other):
    return lax.optimization_barrier((value, other))[0]


def swapped(value, axes):
    return lax.all_to_all(value, axes, 0, 0)


def halved(value):
    high = value.astype(jnp.bfloat16)
    return high, (value - high.astype(jnp.float32)).astype(jnp.bfloat16)


def call(kernel, shapes, in_specs, scratch=(), name=None, mib=12, flops=1000):
    return pl.pallas_call(
        kernel,
        out_shape=shapes,
        in_specs=in_specs,
        out_specs=jax.tree.map(lambda _: VMEM, shapes),
        scratch_shapes=list(scratch),
        compiler_params=pltpu.CompilerParams(vmem_limit_bytes=mib << 20),
        cost_estimate=pl.CostEstimate(flops=flops, bytes_accessed=1000, transcendentals=0),
        name=name,
    )


def f32(*shape):
    return jax.ShapeDtypeStruct(shape, jnp.float32)


def bf16(*shape):
    return jax.ShapeDtypeStruct(shape, jnp.bfloat16)


def products_kernel(order, *refs):
    *blocks, own, other, out, both, basis, done = refs
    total, (own_cols, depth) = out.shape[0], own.shape
    cols = 2 * own_cols
    tiles, copies = [], []
    for start in range(0, cols, TILE):
        end = min(start + TILE, cols)
        tiles.append((start, end, []))
        for ref, base in ((own, 0), (other, own_cols)):
            low, high = max(start - base, 0), min(end - base, own_cols)
            if low < high:
                copy = pltpu.make_async_copy(
                    ref.at[low:high], basis.at[base + low : base + high], done.at[len(copies)]
                )
                copy.start()
                copies.append(copy)
                tiles[-1][2].append(copy)
    at = 0
    for ref in blocks:
        rows = ref.shape[0]
        both[at : at + rows, :], both[total + at : total + at + rows, :] = halved(ref[...])
        at += rows

    def product(a, b):
        return lax.dot_general(
            a, b, (((1,), (1,)), ((), ())), preferred_element_type=jnp.float32
        )

    for start, end, waits in tiles:
        for copy in waits:
            copy.wait()
        high, low = halved(basis[start:end, :])
        main = product(both[...], high)
        out[:, start:end] = main[:total] + (main[total:] + product(both[:total, :], low))


def products(blocks, own, other, order, flops):
    rows = sum(block.shape[0] for block in blocks)
    own_cols, depth = own.shape
    cols = 2 * own_cols
    return call(
        products_kernel,
        f32(rows, cols),
        [VMEM] * (1 + len(blocks)) + [pl.BlockSpec(memory_space=pltpu.HBM)] * 2,
        [
            pltpu.VMEM((2 * rows, depth), jnp.bfloat16),
            pltpu.VMEM((cols, depth), jnp.float32),
            pltpu.SemaphoreType.DMA((cols // TILE + 2,)),
        ],
        name="products",
        mib=22,
        flops=flops,
    )(order, *blocks, own, other)


def sum_kernel(*refs):
    *arrived, out = refs
    at = 0
    for ref in arrived:
        total = ref[0]
        for k in range(1, ref.shape[0]):
            total = total + ref[k]
        rows = total.shape[0]
        for k in range(out.shape[0]):
            out[k, at : at + rows, :] = total
        at += rows


def sum_copies(*arrived):
    n, _, cols = arrived[0].shape
    rows = sum(part.shape[1] for part in arrived)
    return call(sum_kernel, f32(n, rows, cols), [VMEM] * len(arrived), name="sum_copies")(*arrived)


def in_pieces(value, n):
    return value.reshape(n, -1, value.shape[1])


def grads_kernel(place, grads, basis, own, other):
    rows = own.shape[0]
    basis_high, basis_low = halved(basis[...])

    def product(a, b):
        return lax.dot_general(
            a, b, (((0,), (0,)), ((), ())), preferred_element_type=jnp.float32
        )

    for out, half in ((other, 1 - place[1]), (own, place[1])):
        high, low = halved(grads[:, pl.ds(pl.multiple_of(half * rows, rows), rows)])
        out[...] = product(high, basis_high) + (
            product(low, basis_high) + product(high, basis_low)
        )


def add_kernel(a, b, out):
    out[...] = a[...] + b[...]


def split_store(value, high_ref, low_ref, row):
    high = value.astype(jnp.bfloat16)
    rows = pl.ds(pl.multiple_of(row, BLOCK), value.shape[0])
    high_ref[rows, :] = high
    low_ref[rows, :] = (value - high.astype(jnp.float32)).astype(jnp.bfloat16)


def moments_kernel(place, bounds, *refs):
    acts_refs, grads_refs, out = refs[:2], refs[2:4], refs[4]
    acts_high, acts_low, grads_high, grads_low, moment = refs[5:]
    z, core, lo = place[0], place[1], place[2]
    cols = out.shape[0]
    first_rows = 2 * len(FIRST) * BLOCK // 8
    for from_other in range(2):
        of_core = 1 - core if from_other else core
        ref = acts_refs[from_other]
        sides = slice(cols, 2 * cols) if from_other else slice(0, cols)
        blocks = [(distance, far) for distance in FIRST for far in range(2)]
        rest = [(distance, far) for distance in (*SECOND, LAST) for far in range(2)]
        for start, size, listed in ((0, first_rows, blocks), (first_rows, 64 - first_rows, rest)):
            for at, (distance, far) in enumerate(listed):
                parts, row = [], at * BLOCK
                while row < (at + 1) * BLOCK:
                    inner = row % size
                    count = min(size - inner, (at + 1) * BLOCK - row)
                    spot = start + inner
                    parts.append(ref[row // size, spot : spot + count, sides])
                    row += count
                value = parts[0] if len(parts) == 1 else jnp.concatenate(parts, 0)
                xl = 1 - lo if far else lo
                row = ((xl * 8 + lax.rem(z + distance + 8, 8)) * 2 + of_core) * BLOCK
                split_store(value, acts_high, acts_low, row)
        ref = grads_refs[from_other]
        rows = pl.ds(pl.multiple_of(of_core * ref.shape[0], ref.shape[0]), ref.shape[0])
        grads_high[rows, :], grads_low[rows, :] = halved(ref[...])

    def product(a, b):
        return lax.dot_general(
            a, b, (((0,), (0,)), ((), ())), preferred_element_type=jnp.float32
        )

    for seq in range(SEQS):
        first, end = bounds[seq], bounds[seq + 1]
        moment[...] = jnp.zeros_like(moment)

        def block(step, carry):
            rows = pl.ds(pl.multiple_of(step * DEPTH, DEPTH), DEPTH)
            number = step * DEPTH + lax.broadcasted_iota(jnp.int32, (DEPTH, 1), 0)
            mine = (number >= first) & (number < end)
            grads_h = jnp.where(mine, grads_high[rows, :].astype(jnp.float32), 0.0).astype(jnp.bfloat16)
            grads_l = jnp.where(mine, grads_low[rows, :].astype(jnp.float32), 0.0).astype(jnp.bfloat16)
            acts_h, acts_l = acts_high[rows, :], acts_low[rows, :]
            moment[...] += product(acts_h, grads_h) + (
                product(acts_l, grads_h) + product(acts_h, grads_l)
            )
            return carry

        lax.fori_loop(first // DEPTH, (end + DEPTH - 1) // DEPTH, block, 0)
        squared = moment[...] * moment[...]
        if seq == 0:
            out[...] = squared
        elif seq < SEQS - 1:
            out[...] += squared
        else:
            out[...] = (out[...] + squared) * (1.0 / SEQS)


def eigenvalues(place, acts, grads, seq_ids):
    labels = jnp.arange(SEQS + 1, dtype=jnp.int32)
    bounds = jnp.sum((seq_ids[None, :] < labels[:, None]).astype(jnp.int32), axis=1)
    cols, out_cols = acts[0].shape[2] // 2, grads[0].shape[1]
    return call(
        moments_kernel,
        f32(cols, out_cols),
        [SMEM, SMEM] + [VMEM] * (len(acts) + len(grads)),
        [
            pltpu.VMEM((TOKENS, cols), jnp.bfloat16),
            pltpu.VMEM((TOKENS, cols), jnp.bfloat16),
            pltpu.VMEM((TOKENS, out_cols), jnp.bfloat16),
            pltpu.VMEM((TOKENS, out_cols), jnp.bfloat16),
            pltpu.VMEM((cols, out_cols), jnp.float32),
        ],
        name="moments",
        mib=28,
    )(place, bounds, *acts, *grads)


def tied(values, *others):
    held = lax.optimization_barrier((tuple(values), others))
    return list(held[0])


def turn(value):
    return shifted(value[:8, :128], "c")


def per_device(activations, act_basis, grads, grad_basis, seq_ids):
    place = jnp.stack([lax.axis_index("z"), lax.axis_index("c"), lax.axis_index("xl")])
    place = place.astype(jnp.int32)
    half, cols = grads.shape[0] // 2, grad_basis.shape[1]

    basis = (act_basis.T, shifted(act_basis, "c").T)
    own, other = call(
        grads_kernel, [f32(half, cols)] * 2, [SMEM, VMEM, VMEM], name="rotate_grads"
    )(place, grads.T, grad_basis)
    part = call(add_kernel, f32(half, cols), [VMEM, VMEM], name="add")(own, shifted(other, "c"))
    arrived, part = tied([shifted(activations, "xl"), part])
    block = jnp.concatenate([activations, arrived], 0)
    part = lax.psum_scatter(part, "z", tiled=True)

    near = [shifted(block, "z", 1), shifted(block, "z", -1)]
    second = [shifted(near[0], "z", 1), shifted(near[1], "z", -1)]
    third = [shifted(second[0], "z", 1), shifted(second[1], "z", -1)]
    first_products = products([block, *near, *second], *basis, turn(second[0]), 1000)
    first_arrived = swapped(in_pieces(first_products, 8), NARROW)
    third, part = tied([third, part])

    far = [shifted(third[0][:BLOCK], "z", 1), shifted(third[1][BLOCK:], "z", -1)]
    part = part + shifted(part, "xl")
    *far, part = tied([*far, part])
    part = lax.all_gather(part, "z", tiled=True)
    second_products = products([*third, *far], *basis, far[0], 5 * 10**9)
    second_products, first_arrived = tied([second_products, first_arrived])
    second_arrived = swapped(in_pieces(second_products, 8), NARROW)
    acts = swapped(sum_copies(first_arrived, second_arrived), NARROW)
    return eigenvalues(
        place, [acts, shifted(acts, "c")], [part, shifted(part, "c")], seq_ids
    )


def solution(mesh):
    split = Mesh(mesh.devices.reshape(tuple(SIZES.values())), tuple(SIZES))
    return jax.shard_map(
        per_device,
        mesh=split,
        in_specs=(P(WIDE, NARROW), P(NARROW, WIDE), P(None, WIDE), P(WIDE, NARROW), P()),
        out_specs=P(WIDE, NARROW),
        check_vma=False,
    )
```

```python
import functools

import jax
import jax.numpy as jnp
from jax import lax
from jax.experimental import pallas as pl
from jax.experimental.pallas import tpu as pltpu
from jax.sharding import Mesh
from jax.sharding import PartitionSpec as P

SEQS = 4
SIZES = {"xl": 2, "z": 8, "c": 2, "xh": 2, "y": 4}
WIDE = ("xl", "z", "c")
NARROW = ("xh", "y")
TOKENS = 1024
BLOCK = 32
DEPTH = 256
MOST = 56
FIRST, SECOND, LAST = (0, -1, 1, -2, 2), (-3, 3), 4
AROUND = (0, -1, 1, -2, 2, -3, 3, 4)
VMEM = pl.BlockSpec(memory_space=pltpu.VMEM)
SMEM = pl.BlockSpec(memory_space=pltpu.SMEM)


def shifted(value, axis, by=1):
    n = SIZES[axis]
    return lax.ppermute(value, axis, [(i, (i + by) % n) for i in range(n)])


def after(value, other):
    return lax.optimization_barrier((value, other))[0]


def swapped(value, axes):
    return lax.all_to_all(value, axes, 0, 0)


def halved(value):
    high = value.astype(jnp.bfloat16)
    return high, (value - high.astype(jnp.float32)).astype(jnp.bfloat16)


def call(kernel, shapes, in_specs, scratch=(), name=None, mib=12, flops=1000):
    return pl.pallas_call(
        kernel,
        out_shape=shapes,
        in_specs=in_specs,
        out_specs=jax.tree.map(lambda _: VMEM, shapes),
        scratch_shapes=list(scratch),
        compiler_params=pltpu.CompilerParams(vmem_limit_bytes=mib << 20),
        cost_estimate=pl.CostEstimate(flops=flops, bytes_accessed=1000, transcendentals=0),
        name=name,
    )


def f32(*shape):
    return jax.ShapeDtypeStruct(shape, jnp.float32)


def bf16(*shape):
    return jax.ShapeDtypeStruct(shape, jnp.bfloat16)


def basis_kernel(own, other, out):
    rows = own.shape[0]
    for at, ref in enumerate((own, other)):
        into = slice(at * rows, (at + 1) * rows)
        out[0, into, :], out[1, into, :] = halved(ref[...])


def split_basis(own, other):
    rows, depth = own.shape
    return call(
        basis_kernel, bf16(2, 2 * rows, depth), [VMEM, VMEM], name="split_basis", mib=MOST
    )(own, other)


def products_kernel(order, *refs):
    *blocks, basis, out, both, held, done = refs
    total = out.shape[0]
    copies = [
        pltpu.make_async_copy(basis.at[k], held.at[k], done.at[k]) for k in range(2)
    ]
    for copy in copies:
        copy.start()
    at = 0
    for ref in blocks:
        rows = ref.shape[0]
        both[at : at + rows, :], both[total + at : total + at + rows, :] = halved(ref[...])
        at += rows

    def product(a, b):
        return lax.dot_general(
            a, b, (((1,), (1,)), ((), ())), preferred_element_type=jnp.float32
        )

    copies[0].wait()
    main = product(both[...], held[0])
    out[...] = main[:total] + main[total:]
    copies[1].wait()
    out[...] += product(both[:total, :], held[1])


def products(blocks, basis, order, flops):
    rows = sum(block.shape[0] for block in blocks)
    _, cols, depth = basis.shape
    return call(
        products_kernel,
        f32(rows, cols),
        [VMEM] * (1 + len(blocks)) + [pl.BlockSpec(memory_space=pltpu.HBM)],
        [
            pltpu.VMEM((2 * rows, depth), jnp.bfloat16),
            pltpu.VMEM(basis.shape, jnp.bfloat16),
            pltpu.SemaphoreType.DMA((2,)),
        ],
        name="products",
        mib=MOST,
        flops=flops,
    )(order, *blocks, basis)


def sum_kernel(*refs):
    *arrived, out = refs
    at = 0
    for ref in arrived:
        total = ref[0]
        for k in range(1, ref.shape[0]):
            total = total + ref[k]
        rows = total.shape[0]
        for k in range(out.shape[0]):
            out[k, at : at + rows, :] = total
        at += rows


def sum_copies(*arrived):
    n, _, cols = arrived[0].shape
    rows = sum(part.shape[1] for part in arrived)
    return call(sum_kernel, f32(n, rows, cols), [VMEM] * len(arrived), name="sum_copies")(*arrived)


def in_pieces(value, n):
    return value.reshape(n, -1, value.shape[1])


def grads_kernel(place, grads, basis, own, *others):
    rows = own.shape[0]
    basis_high, basis_low = halved(basis[...])

    def product(a, b):
        return lax.dot_general(
            a, b, (((0,), (0,)), ((), ())), preferred_element_type=jnp.float32
        )

    def rotated(half):
        high, low = halved(grads[:, pl.ds(pl.multiple_of(half * rows, rows), rows)])
        return product(high, basis_high) + (
            product(low, basis_high) + product(high, basis_low)
        )

    value = rotated(1 - place[1])
    for k, ref in enumerate(others):
        ref[...] = value[k * ref.shape[0] : (k + 1) * ref.shape[0]]
    own[...] = rotated(place[1])


def add_kernel(own, *refs):
    *arrived, out = refs
    for k, ref in enumerate(arrived):
        rows = slice(k * ref.shape[0], (k + 1) * ref.shape[0])
        out[rows, :] = own[rows, :] + ref[...]


def split_store(value, high_ref, low_ref, row):
    high = value.astype(jnp.bfloat16)
    rows = pl.ds(pl.multiple_of(row, BLOCK), value.shape[0])
    high_ref[rows, :] = high
    low_ref[rows, :] = (value - high.astype(jnp.float32)).astype(jnp.bfloat16)


def moments_kernel(place, bounds, *refs):
    acts_refs, grads_refs, out = refs[:2], refs[2:-6], refs[-6]
    acts_high, acts_low, grads_high, grads_low, moment = refs[-5:]
    z, core, lo = place[0], place[1], place[2]
    cols = out.shape[0]
    first_rows = 2 * len(FIRST) * BLOCK // 8
    for from_other in range(2):
        of_core = 1 - core if from_other else core
        ref = acts_refs[from_other]
        sides = slice(cols, 2 * cols) if from_other else slice(0, cols)
        blocks = [(distance, far) for distance in FIRST for far in range(2)]
        rest = [(distance, far) for distance in (*SECOND, LAST) for far in range(2)]
        for start, size, listed in ((0, first_rows, blocks), (first_rows, 64 - first_rows, rest)):
            for at, (distance, far) in enumerate(listed):
                parts, row = [], at * BLOCK
                while row < (at + 1) * BLOCK:
                    inner = row % size
                    count = min(size - inner, (at + 1) * BLOCK - row)
                    spot = start + inner
                    parts.append(ref[row // size, spot : spot + count, sides])
                    row += count
                value = parts[0] if len(parts) == 1 else jnp.concatenate(parts, 0)
                xl = 1 - lo if far else lo
                row = ((xl * 8 + lax.rem(z + distance + 8, 8)) * 2 + of_core) * BLOCK
                split_store(value, acts_high, acts_low, row)
        for at, distance in enumerate(AROUND):
            ref = grads_refs[at + from_other * len(AROUND)]
            row = of_core * 512 + lax.rem(z + distance + 8, 8) * ref.shape[0]
            split_store(ref[...], grads_high, grads_low, row)

    def product(a, b):
        return lax.dot_general(
            a, b, (((0,), (0,)), ((), ())), preferred_element_type=jnp.float32
        )

    for seq in range(SEQS):
        first, end = bounds[seq], bounds[seq + 1]
        moment[...] = jnp.zeros_like(moment)

        def block(step, carry):
            rows = pl.ds(pl.multiple_of(step * DEPTH, DEPTH), DEPTH)
            number = step * DEPTH + lax.broadcasted_iota(jnp.int32, (DEPTH, 1), 0)
            mine = (number >= first) & (number < end)
            grads_h = jnp.where(mine, grads_high[rows, :].astype(jnp.float32), 0.0).astype(jnp.bfloat16)
            grads_l = jnp.where(mine, grads_low[rows, :].astype(jnp.float32), 0.0).astype(jnp.bfloat16)
            acts_h, acts_l = acts_high[rows, :], acts_low[rows, :]
            moment[...] += product(acts_h, grads_h) + (
                product(acts_l, grads_h) + product(acts_h, grads_l)
            )
            return carry

        lax.fori_loop(first // DEPTH, (end + DEPTH - 1) // DEPTH, block, 0)
        squared = moment[...] * moment[...]
        if seq == 0:
            out[...] = squared
        elif seq < SEQS - 1:
            out[...] += squared
        else:
            out[...] = (out[...] + squared) * (1.0 / SEQS)


def eigenvalues(place, acts, grads, seq_ids):
    labels = jnp.arange(SEQS + 1, dtype=jnp.int32)
    bounds = jnp.sum((seq_ids[None, :] < labels[:, None]).astype(jnp.int32), axis=1)
    cols, out_cols = acts[0].shape[2] // 2, grads[0].shape[1]
    return call(
        moments_kernel,
        f32(cols, out_cols),
        [SMEM, SMEM] + [VMEM] * (len(acts) + len(grads)),
        [
            pltpu.VMEM((TOKENS, cols), jnp.bfloat16),
            pltpu.VMEM((TOKENS, cols), jnp.bfloat16),
            pltpu.VMEM((TOKENS, out_cols), jnp.bfloat16),
            pltpu.VMEM((TOKENS, out_cols), jnp.bfloat16),
            pltpu.VMEM((cols, out_cols), jnp.float32),
        ],
        name="moments",
        mib=28,
    )(place, bounds, *acts, *grads)


def tied(values, *others):
    held = lax.optimization_barrier((tuple(values), others))
    return list(held[0])


def turn(value):
    return shifted(value[:8, :128], "c")


def per_device(activations, act_basis, grads, grad_basis, seq_ids):
    place = jnp.stack([lax.axis_index("z"), lax.axis_index("c"), lax.axis_index("xl")])
    place = place.astype(jnp.int32)
    half, cols = grads.shape[0] // 2, grad_basis.shape[1]

    other_basis = shifted(act_basis, "c").T
    arrived = shifted(activations, "xl")
    own, *others = call(
        grads_kernel,
        [f32(half, cols)] + [f32(half // 8, cols)] * 8,
        [SMEM, VMEM, VMEM],
        name="rotate_grads",
    )(place, grads.T, grad_basis)
    others = [shifted(value, "c") for value in others]
    part = call(add_kernel, f32(half, cols), [VMEM] * 9, name="add")(own, *others)
    arrived, part = tied([arrived, part])
    block = jnp.concatenate([activations, arrived], 0)
    part = lax.psum_scatter(part, "z", tiled=True)

    near = [shifted(block, "z", 1), shifted(block, "z", -1)]
    basis = split_basis(act_basis.T, other_basis)
    *near, basis = tied([*near, basis])
    second = [shifted(near[0], "z", 1), shifted(near[1], "z", -1)]
    third = [shifted(second[0], "z", 1), shifted(second[1], "z", -1)]
    first_products = products([block, *near, *second], basis, turn(second[0]), 1000)
    part = part + shifted(part, "xl")
    first_products, part = tied([first_products, part])
    first_arrived = swapped(in_pieces(first_products, 8), NARROW)

    far = [shifted(third[0][:BLOCK], "z", 1), shifted(third[1][BLOCK:], "z", -1)]
    up1, down1 = shifted(part, "z", 1), shifted(part, "z", -1)
    *far, up1, down1 = tied([*far, up1, down1])
    second_products = products([*third, *far], basis, far[0], 5 * 10**9)
    second_products, first_arrived = tied([second_products, first_arrived])
    second_arrived = swapped(in_pieces(second_products, 8), NARROW)
    up2, down2 = shifted(up1, "z", 1), shifted(down1, "z", -1)
    second_arrived, up2, down2 = tied([second_arrived, up2, down2])
    acts = swapped(sum_copies(first_arrived, second_arrived), NARROW)
    up3, down3 = shifted(up2, "z", 1), shifted(down2, "z", -1)
    parts = [part, up1, down1, up2, down2, up3, down3, shifted(up3, "z", 1)]
    acts, *parts = tied([acts, *parts])
    parts += [shifted(value, "c") for value in parts]
    return eigenvalues(place, [acts, shifted(acts, "c")], parts, seq_ids)


def solution(mesh):
    split = Mesh(mesh.devices.reshape(tuple(SIZES.values())), tuple(SIZES))
    return jax.shard_map(
        per_device,
        mesh=split,
        in_specs=(P(WIDE, NARROW), P(NARROW, WIDE), P(None, WIDE), P(WIDE, NARROW), P()),
        out_specs=P(WIDE, NARROW),
        check_vma=False,
    )
```

```python
import functools

import jax
import jax.numpy as jnp
from jax import lax
from jax.experimental import pallas as pl
from jax.experimental.pallas import tpu as pltpu
from jax.sharding import Mesh
from jax.sharding import PartitionSpec as P

SEQS = 4
SIZES = {"xl": 2, "z": 8, "c": 2, "xh": 2, "y": 4}
WIDE = ("xl", "z", "c")
NARROW = ("xh", "y")
TOKENS = 1024
BLOCK = 32
DEPTH = 256
FIRST, SECOND, LAST = (0, -1, 1, -2, 2), (-3, 3), 4
AROUND = (0, -1, 1, -2, 2, -3, 3, 4)
VMEM = pl.BlockSpec(memory_space=pltpu.VMEM)
SMEM = pl.BlockSpec(memory_space=pltpu.SMEM)


def shifted(value, axis, by=1):
    n = SIZES[axis]
    return lax.ppermute(value, axis, [(i, (i + by) % n) for i in range(n)])


def after(value, other):
    return lax.optimization_barrier((value, other))[0]


def swapped(value, axes):
    return lax.all_to_all(value, axes, 0, 0)


def halved(value):
    high = value.astype(jnp.bfloat16)
    return high, (value - high.astype(jnp.float32)).astype(jnp.bfloat16)


def call(kernel, shapes, in_specs, scratch=(), name=None, mib=12, flops=1000):
    return pl.pallas_call(
        kernel,
        out_shape=shapes,
        in_specs=in_specs,
        out_specs=VMEM if not isinstance(shapes, list) else [VMEM] * len(shapes),
        scratch_shapes=list(scratch),
        compiler_params=pltpu.CompilerParams(vmem_limit_bytes=mib << 20),
        cost_estimate=pl.CostEstimate(flops=flops, bytes_accessed=1000, transcendentals=0),
        name=name,
    )


def f32(*shape):
    return jax.ShapeDtypeStruct(shape, jnp.float32)


def bf16(*shape):
    return jax.ShapeDtypeStruct(shape, jnp.bfloat16)


def basis_kernel(own, other, out):
    rows = own.shape[0]
    for at, ref in enumerate((own, other)):
        into = slice(at * rows, (at + 1) * rows)
        out[0, into, :], out[1, into, :] = halved(ref[...])


def split_basis(own, other):
    rows, depth = own.shape
    return call(
        basis_kernel,
        pltpu.VMEM((2, 2 * rows, depth), jnp.bfloat16),
        [VMEM, VMEM],
        name="split_basis",
    )(own, other)


def products_kernel(*refs):
    *blocks, basis, out, both = refs
    total = out.shape[0]
    at = 0
    for ref in blocks:
        rows = ref.shape[0]
        both[at : at + rows, :], both[total + at : total + at + rows, :] = halved(ref[...])
        at += rows

    def product(a, b):
        return lax.dot_general(
            a, b, (((1,), (1,)), ((), ())), preferred_element_type=jnp.float32
        )

    main = product(both[...], basis[0])
    out[...] = main[:total] + (main[total:] + product(both[:total, :], basis[1]))


def products(blocks, basis, flops):
    rows = sum(block.shape[0] for block in blocks)
    _, cols, depth = basis.shape
    return call(
        products_kernel,
        f32(rows, cols),
        [VMEM] * (1 + len(blocks)),
        [pltpu.VMEM((2 * rows, depth), jnp.bfloat16)],
        name="products",
        mib=16,
        flops=flops,
    )(*blocks, basis)


def sum_kernel(*refs):
    *arrived, out = refs
    at = 0
    for ref in arrived:
        total = ref[0]
        for k in range(1, ref.shape[0]):
            total = total + ref[k]
        rows = total.shape[0]
        for k in range(out.shape[0]):
            out[k, at : at + rows, :] = total
        at += rows


def sum_copies(*arrived, copies=8):
    cols = arrived[0].shape[2]
    rows = sum(part.shape[1] for part in arrived)
    return call(sum_kernel, f32(copies, rows, cols), [VMEM] * len(arrived), name="sum_copies")(*arrived)


def in_pieces(value, n):
    return value.reshape(n, -1, value.shape[1])


def grads_kernel(place, grads, basis, own, other):
    rows = own.shape[0]
    basis_high, basis_low = halved(basis[...])

    def product(a, b):
        return lax.dot_general(
            a, b, (((0,), (0,)), ((), ())), preferred_element_type=jnp.float32
        )

    for out, half in ((other, 1 - place[1]), (own, place[1])):
        high, low = halved(grads[:, pl.ds(pl.multiple_of(half * rows, rows), rows)])
        out[...] = product(high, basis_high) + (
            product(low, basis_high) + product(high, basis_low)
        )


def halves_kernel(place, own, arrived, keep, send):
    rows = keep.shape[0]
    kept = pl.ds(pl.multiple_of(place[2] * rows, rows), rows)
    sent = pl.ds(pl.multiple_of((1 - place[2]) * rows, rows), rows)
    keep[...] = own[kept, :] + arrived[kept, :]
    send[...] = own[sent, :] + arrived[sent, :]


def add_kernel(a, b, out):
    out[...] = a[...] + b[...]


def pair_kernel(place, own, other, out):
    rows = own.shape[1]
    out[pl.ds(pl.multiple_of(place[2] * rows, rows), rows), :] = own[0]
    out[pl.ds(pl.multiple_of((1 - place[2]) * rows, rows), rows), :] = other[0]


def place_kernel(place, *refs):
    *pieces, out = refs
    rows = pieces[0].shape[0] // 2
    for ref, distance in zip(pieces, AROUND):
        row = lax.rem(place[0] + distance + 8, 8) * rows
        for lo in range(2):
            into = pl.ds(pl.multiple_of(lo * 8 * rows + row, rows), rows)
            out[into, :] = ref[lo * rows : (lo + 1) * rows, :]


def split_store(value, high_ref, low_ref, row):
    high = value.astype(jnp.bfloat16)
    rows = pl.ds(pl.multiple_of(row, BLOCK), value.shape[0])
    high_ref[rows, :] = high
    low_ref[rows, :] = (value - high.astype(jnp.float32)).astype(jnp.bfloat16)


def moments_kernel(place, bounds, *refs):
    acts_refs, grads_refs, out = refs[:2], refs[2:-6], refs[-6]
    acts_high, acts_low, grads_high, grads_low, moment = refs[-5:]
    z, core, lo = place[0], place[1], place[2]
    cols = out.shape[0]
    first_rows = 2 * len(FIRST) * BLOCK // 8
    for from_other in range(2):
        of_core = 1 - core if from_other else core
        ref = acts_refs[from_other]
        sides = slice(cols, 2 * cols) if from_other else slice(0, cols)
        blocks = [(distance, far) for distance in FIRST for far in range(2)]
        rest = [(distance, far) for distance in (*SECOND, LAST) for far in range(2)]
        for start, size, listed in ((0, first_rows, blocks), (first_rows, 64 - first_rows, rest)):
            for at, (distance, far) in enumerate(listed):
                parts, row = [], at * BLOCK
                while row < (at + 1) * BLOCK:
                    inner = row % size
                    count = min(size - inner, (at + 1) * BLOCK - row)
                    spot = start + inner
                    parts.append(ref[row // size, spot : spot + count, sides])
                    row += count
                value = parts[0] if len(parts) == 1 else jnp.concatenate(parts, 0)
                xl = 1 - lo if far else lo
                row = ((xl * 8 + lax.rem(z + distance + 8, 8)) * 2 + of_core) * BLOCK
                split_store(value, acts_high, acts_low, row)
        ref = grads_refs[from_other]
        rows = pl.ds(pl.multiple_of(of_core * ref.shape[0], ref.shape[0]), ref.shape[0])
        grads_high[rows, :], grads_low[rows, :] = halved(ref[...])

    def product(a, b):
        return lax.dot_general(
            a, b, (((0,), (0,)), ((), ())), preferred_element_type=jnp.float32
        )

    for seq in range(SEQS):
        first, end = bounds[seq], bounds[seq + 1]
        moment[...] = jnp.zeros_like(moment)

        def block(step, carry):
            rows = pl.ds(pl.multiple_of(step * DEPTH, DEPTH), DEPTH)
            number = step * DEPTH + lax.broadcasted_iota(jnp.int32, (DEPTH, 1), 0)
            mine = (number >= first) & (number < end)
            grads_h = jnp.where(mine, grads_high[rows, :].astype(jnp.float32), 0.0).astype(jnp.bfloat16)
            grads_l = jnp.where(mine, grads_low[rows, :].astype(jnp.float32), 0.0).astype(jnp.bfloat16)
            acts_h, acts_l = acts_high[rows, :], acts_low[rows, :]
            moment[...] += product(acts_h, grads_h) + (
                product(acts_l, grads_h) + product(acts_h, grads_l)
            )
            return carry

        lax.fori_loop(first // DEPTH, (end + DEPTH - 1) // DEPTH, block, 0)
        squared = moment[...] * moment[...]
        if seq == 0:
            out[...] = squared
        elif seq < SEQS - 1:
            out[...] += squared
        else:
            out[...] = (out[...] + squared) * (1.0 / SEQS)


def eigenvalues(place, acts, grads, seq_ids):
    labels = jnp.arange(SEQS + 1, dtype=jnp.int32)
    bounds = jnp.sum((seq_ids[None, :] < labels[:, None]).astype(jnp.int32), axis=1)
    cols, out_cols = acts[0].shape[2] // 2, grads[0].shape[1]
    return call(
        moments_kernel,
        f32(cols, out_cols),
        [SMEM, SMEM] + [VMEM] * (len(acts) + len(grads)),
        [
            pltpu.VMEM((TOKENS, cols), jnp.bfloat16),
            pltpu.VMEM((TOKENS, cols), jnp.bfloat16),
            pltpu.VMEM((TOKENS, out_cols), jnp.bfloat16),
            pltpu.VMEM((TOKENS, out_cols), jnp.bfloat16),
            pltpu.VMEM((cols, out_cols), jnp.float32),
        ],
        name="moments",
        mib=28,
    )(place, bounds, *acts, *grads)


def tied(values, *others):
    held = lax.optimization_barrier((tuple(values), others))
    return list(held[0])


def per_device(activations, act_basis, grads, grad_basis, seq_ids):
    place = jnp.stack([lax.axis_index("z"), lax.axis_index("c"), lax.axis_index("xl")])
    place = place.astype(jnp.int32)
    half, cols = grads.shape[0] // 2, grad_basis.shape[1]

    def placed(kernel, shapes, name, *values):
        specs = [SMEM] + [VMEM] * len(values)
        return call(kernel, shapes, specs, name=name)(place, *values)

    other_basis = shifted(act_basis, "c").T
    arrived = shifted(activations, "xl")
    own, other = placed(
        grads_kernel, [f32(half, cols)] * 2, "rotate_grads", grads.T, grad_basis
    )
    keep, send = placed(
        halves_kernel, [f32(half // 2, cols)] * 2, "add_halves", own, shifted(other, "c")
    )
    arrived, keep, send = tied([arrived, keep, send])
    block = jnp.concatenate([activations, arrived], 0)

    near = [shifted(block, "z", 1), shifted(block, "z", -1)]
    basis = split_basis(act_basis.T, other_basis)
    part = call(add_kernel, f32(half // 2, cols), [VMEM, VMEM], name="add")(
        keep, shifted(send, "xl")
    )
    *near, basis = tied([*near, basis])
    part_arrived = swapped(in_pieces(part, 8), "z")
    second = [shifted(near[0], "z", 1), shifted(near[1], "z", -1)]
    third = [shifted(second[0], "z", 1), shifted(second[1], "z", -1)]
    first_products = products([block, *near, *second], basis, 1000)
    first_products, part_arrived = tied([first_products, part_arrived])
    first_arrived = swapped(in_pieces(first_products, 8), NARROW)

    far = [shifted(third[0][:BLOCK], "z", 1), shifted(third[1][BLOCK:], "z", -1)]
    second_products = products([*third, *far], basis, 5 * 10**9)
    piece = sum_copies(part_arrived, copies=1)
    part = placed(
        pair_kernel, f32(2 * piece.shape[1], cols), "pair", piece, shifted(piece, "xl")
    )
    second_products, first_arrived, part = tied([second_products, first_arrived, part])
    second_arrived = swapped(in_pieces(second_products, 8), NARROW)

    up1, down1 = shifted(part, "z", 1), shifted(part, "z", -1)
    second_arrived, up1, down1 = tied([second_arrived, up1, down1])
    acts = swapped(sum_copies(first_arrived, second_arrived), NARROW)
    up2, down2 = shifted(up1, "z", 1), shifted(down1, "z", -1)
    up3, down3 = shifted(up2, "z", 1), shifted(down2, "z", -1)
    parts = [part, up1, down1, up2, down2, up3, down3, shifted(up3, "z", 1)]
    part = placed(place_kernel, f32(half, cols), "place", *parts)
    acts, part = tied([acts, part])
    return eigenvalues(
        place, [acts, shifted(acts, "c")], [part, shifted(part, "c")], seq_ids
    )


def solution(mesh):
    split = Mesh(mesh.devices.reshape(tuple(SIZES.values())), tuple(SIZES))
    return jax.shard_map(
        per_device,
        mesh=split,
        in_specs=(P(WIDE, NARROW), P(NARROW, WIDE), P(None, WIDE), P(WIDE, NARROW), P()),
        out_specs=P(WIDE, NARROW),
        check_vma=False,
    )
```

```python
import functools

import jax
import jax.numpy as jnp
from jax import lax
from jax.experimental import pallas as pl
from jax.experimental.pallas import tpu as pltpu
from jax.sharding import Mesh
from jax.sharding import PartitionSpec as P

SEQS = 4
SIZES = {"xl": 2, "z": 8, "c": 2, "xh": 2, "y": 4}
WIDE = ("xl", "z", "c")
NARROW = ("xh", "y")
TOKENS = 1024
BLOCK = 32
DEPTH = 256
FIRST, SECOND, LAST = (0, -1, 1, -2, 2), (-3, 3), 4
AROUND = (0, -1, 1, -2, 2, -3, 3, 4)
VMEM = pl.BlockSpec(memory_space=pltpu.VMEM)
SMEM = pl.BlockSpec(memory_space=pltpu.SMEM)


def shifted(value, axis, by=1):
    n = SIZES[axis]
    return lax.ppermute(value, axis, [(i, (i + by) % n) for i in range(n)])


def after(value, other):
    return lax.optimization_barrier((value, other))[0]


def swapped(value, axes):
    return lax.all_to_all(value, axes, 0, 0)


def halved(value):
    high = value.astype(jnp.bfloat16)
    return high, (value - high.astype(jnp.float32)).astype(jnp.bfloat16)


def call(kernel, shapes, in_specs, scratch=(), name=None, mib=12, flops=1000):
    return pl.pallas_call(
        kernel,
        out_shape=shapes,
        in_specs=in_specs,
        out_specs=VMEM if not isinstance(shapes, list) else [VMEM] * len(shapes),
        scratch_shapes=list(scratch),
        compiler_params=pltpu.CompilerParams(vmem_limit_bytes=mib << 20),
        cost_estimate=pl.CostEstimate(flops=flops, bytes_accessed=1000, transcendentals=0),
        name=name,
    )


def f32(*shape):
    return jax.ShapeDtypeStruct(shape, jnp.float32)


def bf16(*shape):
    return jax.ShapeDtypeStruct(shape, jnp.bfloat16)


def basis_kernel(own, other, out):
    rows = own.shape[0]
    for at, ref in enumerate((own, other)):
        into = slice(at * rows, (at + 1) * rows)
        out[0, into, :], out[1, into, :] = halved(ref[...])


def split_basis(own, other):
    rows, depth = own.shape
    return call(
        basis_kernel,
        pltpu.VMEM((2, 2 * rows, depth), jnp.bfloat16),
        [VMEM, VMEM],
        name="split_basis",
    )(own, other)


def products_kernel(*refs):
    *blocks, basis, out, both = refs
    total = out.shape[0]
    at = 0
    for ref in blocks:
        rows = ref.shape[0]
        both[at : at + rows, :], both[total + at : total + at + rows, :] = halved(ref[...])
        at += rows

    def product(a, b):
        return lax.dot_general(
            a, b, (((1,), (1,)), ((), ())), preferred_element_type=jnp.float32
        )

    main = product(both[...], basis[0])
    out[...] = main[:total] + (main[total:] + product(both[:total, :], basis[1]))


def products(blocks, basis, flops):
    rows = sum(block.shape[0] for block in blocks)
    _, cols, depth = basis.shape
    return call(
        products_kernel,
        f32(rows, cols),
        [VMEM] * (1 + len(blocks)),
        [pltpu.VMEM((2 * rows, depth), jnp.bfloat16)],
        name="products",
        mib=16,
        flops=flops,
    )(*blocks, basis)


def sum_kernel(*refs):
    *arrived, out = refs
    at = 0
    for ref in arrived:
        total = ref[0]
        for k in range(1, ref.shape[0]):
            total = total + ref[k]
        rows = total.shape[0]
        for k in range(out.shape[0]):
            out[k, at : at + rows, :] = total
        at += rows


def sum_copies(*arrived, copies=8):
    cols = arrived[0].shape[2]
    rows = sum(part.shape[1] for part in arrived)
    return call(sum_kernel, f32(copies, rows, cols), [VMEM] * len(arrived), name="sum_copies")(*arrived)


def in_pieces(value, n):
    return value.reshape(n, -1, value.shape[1])


def grads_kernel(place, grads, basis, own, other):
    rows = own.shape[0]
    basis_high, basis_low = halved(basis[...])

    def product(a, b):
        return lax.dot_general(
            a, b, (((0,), (0,)), ((), ())), preferred_element_type=jnp.float32
        )

    for out, half in ((other, 1 - place[1]), (own, place[1])):
        high, low = halved(grads[:, pl.ds(pl.multiple_of(half * rows, rows), rows)])
        out[...] = product(high, basis_high) + (
            product(low, basis_high) + product(high, basis_low)
        )


def halves_kernel(place, own, arrived, keep, send):
    rows = keep.shape[0]
    kept = pl.ds(pl.multiple_of(place[2] * rows, rows), rows)
    sent = pl.ds(pl.multiple_of((1 - place[2]) * rows, rows), rows)
    keep[...] = own[kept, :] + arrived[kept, :]
    send[...] = own[sent, :] + arrived[sent, :]


def add_kernel(a, b, out):
    out[...] = a[...] + b[...]


def pair_kernel(place, own, other, out):
    rows = own.shape[1]
    out[pl.ds(pl.multiple_of(place[2] * rows, rows), rows), :] = own[0]
    out[pl.ds(pl.multiple_of((1 - place[2]) * rows, rows), rows), :] = other[0]


def place_kernel(place, *refs):
    *pieces, out = refs
    rows = pieces[0].shape[0] // 2
    for ref, distance in zip(pieces, AROUND):
        row = lax.rem(place[0] + distance + 8, 8) * rows
        for lo in range(2):
            into = pl.ds(pl.multiple_of(lo * 8 * rows + row, rows), rows)
            out[into, :] = ref[lo * rows : (lo + 1) * rows, :]


def split_store(value, high_ref, low_ref, row):
    high = value.astype(jnp.bfloat16)
    rows = pl.ds(pl.multiple_of(row, BLOCK), value.shape[0])
    high_ref[rows, :] = high
    low_ref[rows, :] = (value - high.astype(jnp.float32)).astype(jnp.bfloat16)


def moments_kernel(place, bounds, *refs):
    acts_refs, grads_refs, out = refs[:2], refs[2:-6], refs[-6]
    acts_high, acts_low, grads_high, grads_low, moment = refs[-5:]
    z, core, lo = place[0], place[1], place[2]
    cols = out.shape[0]
    first_rows = 2 * len(FIRST) * BLOCK // 8
    for from_other in range(2):
        of_core = 1 - core if from_other else core
        ref = acts_refs[from_other]
        sides = slice(cols, 2 * cols) if from_other else slice(0, cols)
        blocks = [(distance, far) for distance in FIRST for far in range(2)]
        rest = [(distance, far) for distance in (*SECOND, LAST) for far in range(2)]
        for start, size, listed in ((0, first_rows, blocks), (first_rows, 64 - first_rows, rest)):
            for at, (distance, far) in enumerate(listed):
                parts, row = [], at * BLOCK
                while row < (at + 1) * BLOCK:
                    inner = row % size
                    count = min(size - inner, (at + 1) * BLOCK - row)
                    spot = start + inner
                    parts.append(ref[row // size, spot : spot + count, sides])
                    row += count
                value = parts[0] if len(parts) == 1 else jnp.concatenate(parts, 0)
                xl = 1 - lo if far else lo
                row = ((xl * 8 + lax.rem(z + distance + 8, 8)) * 2 + of_core) * BLOCK
                split_store(value, acts_high, acts_low, row)
        ref = grads_refs[from_other]
        rows = pl.ds(pl.multiple_of(of_core * ref.shape[0], ref.shape[0]), ref.shape[0])
        grads_high[rows, :], grads_low[rows, :] = halved(ref[...])

    def product(a, b):
        return lax.dot_general(
            a, b, (((0,), (0,)), ((), ())), preferred_element_type=jnp.float32
        )

    for seq in range(SEQS):
        first, end = bounds[seq], bounds[seq + 1]
        moment[...] = jnp.zeros_like(moment)

        def block(step, carry):
            rows = pl.ds(pl.multiple_of(step * DEPTH, DEPTH), DEPTH)
            number = step * DEPTH + lax.broadcasted_iota(jnp.int32, (DEPTH, 1), 0)
            mine = (number >= first) & (number < end)
            grads_h = jnp.where(mine, grads_high[rows, :].astype(jnp.float32), 0.0).astype(jnp.bfloat16)
            grads_l = jnp.where(mine, grads_low[rows, :].astype(jnp.float32), 0.0).astype(jnp.bfloat16)
            acts_h, acts_l = acts_high[rows, :], acts_low[rows, :]
            moment[...] += product(acts_h, grads_h) + (
                product(acts_l, grads_h) + product(acts_h, grads_l)
            )
            return carry

        lax.fori_loop(first // DEPTH, (end + DEPTH - 1) // DEPTH, block, 0)
        squared = moment[...] * moment[...]
        if seq == 0:
            out[...] = squared
        elif seq < SEQS - 1:
            out[...] += squared
        else:
            out[...] = (out[...] + squared) * (1.0 / SEQS)


def eigenvalues(place, acts, grads, seq_ids):
    labels = jnp.arange(SEQS + 1, dtype=jnp.int32)
    bounds = jnp.sum((seq_ids[None, :] < labels[:, None]).astype(jnp.int32), axis=1)
    cols, out_cols = acts[0].shape[2] // 2, grads[0].shape[1]
    return call(
        moments_kernel,
        f32(cols, out_cols),
        [SMEM, SMEM] + [VMEM] * (len(acts) + len(grads)),
        [
            pltpu.VMEM((TOKENS, cols), jnp.bfloat16),
            pltpu.VMEM((TOKENS, cols), jnp.bfloat16),
            pltpu.VMEM((TOKENS, out_cols), jnp.bfloat16),
            pltpu.VMEM((TOKENS, out_cols), jnp.bfloat16),
            pltpu.VMEM((cols, out_cols), jnp.float32),
        ],
        name="moments",
        mib=28,
    )(place, bounds, *acts, *grads)


def tied(values, *others):
    held = lax.optimization_barrier((tuple(values), others))
    return list(held[0])


def per_device(activations, act_basis, grads, grad_basis, seq_ids):
    place = jnp.stack([lax.axis_index("z"), lax.axis_index("c"), lax.axis_index("xl")])
    place = place.astype(jnp.int32)
    half, cols = grads.shape[0] // 2, grad_basis.shape[1]

    def placed(kernel, shapes, name, *values):
        specs = [SMEM] + [VMEM] * len(values)
        return call(kernel, shapes, specs, name=name)(place, *values)

    other_basis = shifted(act_basis, "c").T
    arrived = shifted(activations, "xl")
    own, other = placed(
        grads_kernel, [f32(half, cols)] * 2, "rotate_grads", grads.T, grad_basis
    )
    arrived, own, other = tied([arrived, own, other])
    block = jnp.concatenate([activations, arrived], 0)
    keep, send = placed(
        halves_kernel, [f32(half // 2, cols)] * 2, "add_halves", own, shifted(other, "c")
    )

    near = [shifted(block, "z", 1), shifted(block, "z", -1)]
    part = call(add_kernel, f32(half // 2, cols), [VMEM, VMEM], name="add")(
        keep, shifted(send, "xl")
    )
    part_arrived = swapped(in_pieces(part, 8), "z")
    second = [shifted(near[0], "z", 1), shifted(near[1], "z", -1)]
    basis = split_basis(*tied([act_basis.T, other_basis], near[0]))
    *second, basis = tied([*second, basis])
    third = [shifted(second[0], "z", 1), shifted(second[1], "z", -1)]
    first_products = products([block, *near, *second], basis, 1000)
    first_products, part_arrived = tied([first_products, part_arrived])
    first_arrived = swapped(in_pieces(first_products, 8), NARROW)

    far = [shifted(third[0][:BLOCK], "z", 1), shifted(third[1][BLOCK:], "z", -1)]
    basis = split_basis(*tied([act_basis.T, other_basis], third[0]))
    *far, basis = tied([*far, basis])
    second_products = products([*third, *far], basis, 5 * 10**9)
    piece = sum_copies(part_arrived, copies=1)
    far_piece, second_products = tied([shifted(piece, "xl"), second_products])
    part = placed(pair_kernel, f32(2 * piece.shape[1], cols), "pair", piece, far_piece)
    second_products, first_arrived, part = tied([second_products, first_arrived, part])
    second_arrived = swapped(in_pieces(second_products, 8), NARROW)

    up1, down1 = shifted(part, "z", 1), shifted(part, "z", -1)
    second_arrived, up1, down1 = tied([second_arrived, up1, down1])
    acts = swapped(sum_copies(first_arrived, second_arrived), NARROW)
    up2, down2 = shifted(up1, "z", 1), shifted(down1, "z", -1)
    up3, down3 = shifted(up2, "z", 1), shifted(down2, "z", -1)
    parts = [part, up1, down1, up2, down2, up3, down3, shifted(up3, "z", 1)]
    part = placed(place_kernel, f32(half, cols), "place", *parts)
    acts, *parts = tied([acts, part, shifted(part, "c")])
    return eigenvalues(place, [acts, shifted(acts, "c")], parts, seq_ids)


def solution(mesh):
    split = Mesh(mesh.devices.reshape(tuple(SIZES.values())), tuple(SIZES))
    return jax.shard_map(
        per_device,
        mesh=split,
        in_specs=(P(WIDE, NARROW), P(NARROW, WIDE), P(None, WIDE), P(WIDE, NARROW), P()),
        out_specs=P(WIDE, NARROW),
        check_vma=False,
    )
```

```python
import functools

import jax
import jax.numpy as jnp
from jax import lax
from jax.experimental import pallas as pl
from jax.experimental.pallas import tpu as pltpu
from jax.sharding import Mesh
from jax.sharding import PartitionSpec as P

SEQS = 4
SIZES = {"xl": 2, "z": 8, "c": 2, "xh": 2, "y": 4}
WIDE = ("xl", "z", "c")
NARROW = ("xh", "y")
TOKENS = 1024
BLOCK = 32
DEPTH = 256
FIRST, SECOND, LAST = (0, -1, 1, -2, 2), (-3, 3), 4
AROUND = (0, -1, 1, -2, 2, -3, 3, 4)
VMEM = pl.BlockSpec(memory_space=pltpu.VMEM)
SMEM = pl.BlockSpec(memory_space=pltpu.SMEM)


def shifted(value, axis, by=1):
    n = SIZES[axis]
    return lax.ppermute(value, axis, [(i, (i + by) % n) for i in range(n)])


def after(value, other):
    return lax.optimization_barrier((value, other))[0]


def swapped(value, axes):
    return lax.all_to_all(value, axes, 0, 0)


def halved(value):
    high = value.astype(jnp.bfloat16)
    return high, (value - high.astype(jnp.float32)).astype(jnp.bfloat16)


def call(kernel, shapes, in_specs, scratch=(), name=None, mib=12, flops=1000):
    return pl.pallas_call(
        kernel,
        out_shape=shapes,
        in_specs=in_specs,
        out_specs=VMEM if not isinstance(shapes, list) else [VMEM] * len(shapes),
        scratch_shapes=list(scratch),
        compiler_params=pltpu.CompilerParams(vmem_limit_bytes=mib << 20),
        cost_estimate=pl.CostEstimate(flops=flops, bytes_accessed=1000, transcendentals=0),
        name=name,
    )


def f32(*shape):
    return jax.ShapeDtypeStruct(shape, jnp.float32)


def bf16(*shape):
    return jax.ShapeDtypeStruct(shape, jnp.bfloat16)


def basis_kernel(own, other, out):
    rows = own.shape[0]
    for at, ref in enumerate((own, other)):
        into = slice(at * rows, (at + 1) * rows)
        out[0, into, :], out[1, into, :] = halved(ref[...])


def split_basis(own, other):
    rows, depth = own.shape
    return call(
        basis_kernel,
        pltpu.VMEM((2, 2 * rows, depth), jnp.bfloat16),
        [VMEM, VMEM],
        name="split_basis",
    )(own, other)


def products_kernel(*refs):
    *blocks, basis, out, both = refs
    total = out.shape[0]
    at = 0
    for ref in blocks:
        rows = ref.shape[0]
        both[at : at + rows, :], both[total + at : total + at + rows, :] = halved(ref[...])
        at += rows

    def product(a, b):
        return lax.dot_general(
            a, b, (((1,), (1,)), ((), ())), preferred_element_type=jnp.float32
        )

    main = product(both[...], basis[0])
    out[...] = main[:total] + (main[total:] + product(both[:total, :], basis[1]))


def products(blocks, basis, flops):
    rows = sum(block.shape[0] for block in blocks)
    _, cols, depth = basis.shape
    return call(
        products_kernel,
        f32(rows, cols),
        [VMEM] * (1 + len(blocks)),
        [pltpu.VMEM((2 * rows, depth), jnp.bfloat16)],
        name="products",
        mib=16,
        flops=flops,
    )(*blocks, basis)


def sum_kernel(*refs):
    *arrived, out = refs
    at = 0
    for ref in arrived:
        total = ref[0]
        for k in range(1, ref.shape[0]):
            total = total + ref[k]
        rows = total.shape[0]
        for k in range(out.shape[0]):
            out[k, at : at + rows, :] = total
        at += rows


def sum_copies(*arrived, copies=8):
    cols = arrived[0].shape[2]
    rows = sum(part.shape[1] for part in arrived)
    return call(sum_kernel, f32(copies, rows, cols), [VMEM] * len(arrived), name="sum_copies")(*arrived)


def in_pieces(value, n):
    return value.reshape(n, -1, value.shape[1])


def grads_kernel(place, grads, basis, own, other):
    rows = own.shape[0]
    basis_high, basis_low = halved(basis[...])

    def product(a, b):
        return lax.dot_general(
            a, b, (((0,), (0,)), ((), ())), preferred_element_type=jnp.float32
        )

    for out, half in ((other, 1 - place[1]), (own, place[1])):
        high, low = halved(grads[:, pl.ds(pl.multiple_of(half * rows, rows), rows)])
        out[...] = product(high, basis_high) + (
            product(low, basis_high) + product(high, basis_low)
        )


def halves_kernel(place, own, arrived, keep, send):
    rows = keep.shape[0]
    kept = pl.ds(pl.multiple_of(place[2] * rows, rows), rows)
    sent = pl.ds(pl.multiple_of((1 - place[2]) * rows, rows), rows)
    keep[...] = own[kept, :] + arrived[kept, :]
    send[...] = own[sent, :] + arrived[sent, :]


def add_kernel(a, b, out):
    out[...] = a[...] + b[...]


def pair_kernel(place, own, other, out):
    rows = own.shape[1]
    out[pl.ds(pl.multiple_of(place[2] * rows, rows), rows), :] = own[0]
    out[pl.ds(pl.multiple_of((1 - place[2]) * rows, rows), rows), :] = other[0]


def place_kernel(place, *refs):
    *pieces, out = refs
    rows = pieces[0].shape[0] // 2
    for ref, distance in zip(pieces, AROUND):
        row = lax.rem(place[0] + distance + 8, 8) * rows
        for lo in range(2):
            into = pl.ds(pl.multiple_of(lo * 8 * rows + row, rows), rows)
            out[into, :] = ref[lo * rows : (lo + 1) * rows, :]


def split_store(value, high_ref, low_ref, row):
    high = value.astype(jnp.bfloat16)
    rows = pl.ds(pl.multiple_of(row, BLOCK), value.shape[0])
    high_ref[rows, :] = high
    low_ref[rows, :] = (value - high.astype(jnp.float32)).astype(jnp.bfloat16)


def split_grads_kernel(place, own, other, high, low):
    rows = own.shape[0]
    for ref, core in ((own, place[1]), (other, 1 - place[1])):
        into = pl.ds(pl.multiple_of(core * rows, rows), rows)
        high[into, :], low[into, :] = halved(ref[...])


def moments_kernel(place, bounds, *refs):
    acts_refs, (grads_high, grads_low, out) = refs[:2], refs[2:5]
    acts_high, acts_low, turned_high, turned_low, moment = refs[5:]
    z, core, lo = place[0], place[1], place[2]
    cols = out.shape[0]
    first_rows = 2 * len(FIRST) * BLOCK // 8
    for from_other in range(2):
        of_core = 1 - core if from_other else core
        ref = acts_refs[from_other]
        sides = slice(cols, 2 * cols) if from_other else slice(0, cols)
        blocks = [(distance, far) for distance in FIRST for far in range(2)]
        rest = [(distance, far) for distance in (*SECOND, LAST) for far in range(2)]
        for start, size, listed in ((0, first_rows, blocks), (first_rows, 64 - first_rows, rest)):
            for at, (distance, far) in enumerate(listed):
                parts, row = [], at * BLOCK
                while row < (at + 1) * BLOCK:
                    inner = row % size
                    count = min(size - inner, (at + 1) * BLOCK - row)
                    spot = start + inner
                    parts.append(ref[row // size, spot : spot + count, sides])
                    row += count
                value = parts[0] if len(parts) == 1 else jnp.concatenate(parts, 0)
                xl = 1 - lo if far else lo
                row = ((xl * 8 + lax.rem(z + distance + 8, 8)) * 2 + of_core) * BLOCK
                split_store(value, acts_high, acts_low, row)
    for start in range(0, TOKENS, DEPTH):
        rows = slice(start, start + DEPTH)
        for ref, turned in ((acts_high, turned_high), (acts_low, turned_low)):
            turned[:, rows] = ref[rows, :].T

    def product(a, b):
        return lax.dot_general(
            a, b, (((1,), (0,)), ((), ())), preferred_element_type=jnp.float32
        )

    for seq in range(SEQS):
        first, end = bounds[seq], bounds[seq + 1]
        moment[...] = jnp.zeros_like(moment)

        def block(step, carry):
            rows = pl.ds(pl.multiple_of(step * DEPTH, DEPTH), DEPTH)
            number = step * DEPTH + lax.broadcasted_iota(jnp.int32, (DEPTH, 1), 0)
            mine = (number >= first) & (number < end)
            grads_h = jnp.where(mine, grads_high[rows, :].astype(jnp.float32), 0.0).astype(jnp.bfloat16)
            grads_l = jnp.where(mine, grads_low[rows, :].astype(jnp.float32), 0.0).astype(jnp.bfloat16)
            acts_h, acts_l = turned_high[:, rows], turned_low[:, rows]
            moment[...] += product(acts_h, grads_h) + (
                product(acts_l, grads_h) + product(acts_h, grads_l)
            )
            return carry

        lax.fori_loop(first // DEPTH, (end + DEPTH - 1) // DEPTH, block, 0)
        squared = moment[...] * moment[...]
        if seq == 0:
            out[...] = squared
        elif seq < SEQS - 1:
            out[...] += squared
        else:
            out[...] = (out[...] + squared) * (1.0 / SEQS)


def eigenvalues(place, acts, grads, seq_ids):
    labels = jnp.arange(SEQS + 1, dtype=jnp.int32)
    bounds = jnp.sum((seq_ids[None, :] < labels[:, None]).astype(jnp.int32), axis=1)
    cols, out_cols = acts[0].shape[2] // 2, grads[0].shape[1]
    grads = call(
        split_grads_kernel,
        [bf16(TOKENS, out_cols)] * 2,
        [SMEM, VMEM, VMEM],
        name="split_grads",
    )(place, *grads)
    return call(
        moments_kernel,
        f32(cols, out_cols),
        [SMEM, SMEM] + [VMEM] * (len(acts) + len(grads)),
        [
            pltpu.VMEM((TOKENS, cols), jnp.bfloat16),
            pltpu.VMEM((TOKENS, cols), jnp.bfloat16),
            pltpu.VMEM((cols, TOKENS), jnp.bfloat16),
            pltpu.VMEM((cols, TOKENS), jnp.bfloat16),
            pltpu.VMEM((cols, out_cols), jnp.float32),
        ],
        name="moments",
        mib=28,
    )(place, bounds, *acts, *grads)


def tied(values, *others):
    held = lax.optimization_barrier((tuple(values), others))
    return list(held[0])


def per_device(activations, act_basis, grads, grad_basis, seq_ids):
    place = jnp.stack([lax.axis_index("z"), lax.axis_index("c"), lax.axis_index("xl")])
    place = place.astype(jnp.int32)
    half, cols = grads.shape[0] // 2, grad_basis.shape[1]

    def placed(kernel, shapes, name, *values):
        specs = [SMEM] + [VMEM] * len(values)
        return call(kernel, shapes, specs, name=name)(place, *values)

    other_basis = shifted(act_basis, "c").T
    arrived = shifted(activations, "xl")
    own, other = placed(
        grads_kernel, [f32(half, cols)] * 2, "rotate_grads", grads.T, grad_basis
    )
    arrived, own, other = tied([arrived, own, other])
    block = jnp.concatenate([activations, arrived], 0)
    keep, send = placed(
        halves_kernel, [f32(half // 2, cols)] * 2, "add_halves", own, shifted(other, "c")
    )

    near = [shifted(block, "z", 1), shifted(block, "z", -1)]
    part = call(add_kernel, f32(half // 2, cols), [VMEM, VMEM], name="add")(
        keep, shifted(send, "xl")
    )
    part_arrived = swapped(in_pieces(part, 8), "z")
    second = [shifted(near[0], "z", 1), shifted(near[1], "z", -1)]
    basis = split_basis(*tied([act_basis.T, other_basis], near[0]))
    *second, basis = tied([*second, basis])
    third = [shifted(second[0], "z", 1), shifted(second[1], "z", -1)]
    first_products = products([block, *near, *second], basis, 1000)
    first_products, part_arrived = tied([first_products, part_arrived])
    first_arrived = swapped(in_pieces(first_products, 8), NARROW)

    far = [shifted(third[0][:BLOCK], "z", 1), shifted(third[1][BLOCK:], "z", -1)]
    basis = split_basis(*tied([act_basis.T, other_basis], third[0]))
    *far, basis = tied([*far, basis])
    second_products = products([*third, *far], basis, 5 * 10**9)
    piece = sum_copies(part_arrived, copies=1)
    far_piece, second_products = tied([shifted(piece, "xl"), second_products])
    part = placed(pair_kernel, f32(2 * piece.shape[1], cols), "pair", piece, far_piece)
    second_products, first_arrived, part = tied([second_products, first_arrived, part])
    second_arrived = swapped(in_pieces(second_products, 8), NARROW)

    up1, down1 = shifted(part, "z", 1), shifted(part, "z", -1)
    second_arrived, up1, down1 = tied([second_arrived, up1, down1])
    acts = swapped(sum_copies(first_arrived, second_arrived), NARROW)
    up2, down2 = shifted(up1, "z", 1), shifted(down1, "z", -1)
    up3, down3 = shifted(up2, "z", 1), shifted(down2, "z", -1)
    parts = [part, up1, down1, up2, down2, up3, down3, shifted(up3, "z", 1)]
    part = placed(place_kernel, f32(half, cols), "place", *parts)
    acts, *parts = tied([acts, part, shifted(part, "c")])
    return eigenvalues(place, [acts, shifted(acts, "c")], parts, seq_ids)


def solution(mesh):
    split = Mesh(mesh.devices.reshape(tuple(SIZES.values())), tuple(SIZES))
    return jax.shard_map(
        per_device,
        mesh=split,
        in_specs=(P(WIDE, NARROW), P(NARROW, WIDE), P(None, WIDE), P(WIDE, NARROW), P()),
        out_specs=P(WIDE, NARROW),
        check_vma=False,
    )
```

```python
import functools

import jax
import jax.numpy as jnp
from jax import lax
from jax.experimental import pallas as pl
from jax.experimental.pallas import tpu as pltpu
from jax.sharding import Mesh
from jax.sharding import PartitionSpec as P

SEQS = 4
SIZES = {"xl": 2, "z": 8, "c": 2, "xh": 2, "y": 4}
WIDE = ("xl", "z", "c")
NARROW = ("xh", "y")
TOKENS = 1024
BLOCK = 32
DEPTH = 256
FIRST, SECOND, LAST = (0, -1, 1, -2, 2), (-3, 3), 4
AROUND = (0, -1, 1, -2, 2, -3, 3, 4)
VMEM = pl.BlockSpec(memory_space=pltpu.VMEM)
SMEM = pl.BlockSpec(memory_space=pltpu.SMEM)


def shifted(value, axis, by=1):
    n = SIZES[axis]
    return lax.ppermute(value, axis, [(i, (i + by) % n) for i in range(n)])


def after(value, other):
    return lax.optimization_barrier((value, other))[0]


def swapped(value, axes):
    return lax.all_to_all(value, axes, 0, 0)


def halved(value):
    high = value.astype(jnp.bfloat16)
    return high, (value - high.astype(jnp.float32)).astype(jnp.bfloat16)


def call(kernel, shapes, in_specs, scratch=(), name=None, mib=12, flops=1000):
    return pl.pallas_call(
        kernel,
        out_shape=shapes,
        in_specs=in_specs,
        out_specs=VMEM if not isinstance(shapes, list) else [VMEM] * len(shapes),
        scratch_shapes=list(scratch),
        compiler_params=pltpu.CompilerParams(vmem_limit_bytes=mib << 20),
        cost_estimate=pl.CostEstimate(flops=flops, bytes_accessed=1000, transcendentals=0),
        name=name,
    )


def f32(*shape):
    return jax.ShapeDtypeStruct(shape, jnp.float32)


def bf16(*shape):
    return jax.ShapeDtypeStruct(shape, jnp.bfloat16)


def basis_kernel(own, other, out):
    rows = own.shape[0]
    for at, ref in enumerate((own, other)):
        into = slice(at * rows, (at + 1) * rows)
        out[0, into, :], out[1, into, :] = halved(ref[...])


def split_basis(own, other):
    rows, depth = own.shape
    return call(
        basis_kernel,
        pltpu.VMEM((2, 2 * rows, depth), jnp.bfloat16),
        [VMEM, VMEM],
        name="split_basis",
    )(own, other)


def products_kernel(*refs):
    *blocks, basis, out, both = refs
    total = out.shape[0]
    at = 0
    for ref in blocks:
        rows = ref.shape[0]
        both[at : at + rows, :], both[total + at : total + at + rows, :] = halved(ref[...])
        at += rows

    def product(a, b):
        return lax.dot_general(
            a, b, (((1,), (1,)), ((), ())), preferred_element_type=jnp.float32
        )

    main = product(both[...], basis[0])
    out[...] = main[:total] + (main[total:] + product(both[:total, :], basis[1]))


def products(blocks, basis, flops):
    rows = sum(block.shape[0] for block in blocks)
    _, cols, depth = basis.shape
    return call(
        products_kernel,
        f32(rows, cols),
        [VMEM] * (1 + len(blocks)),
        [pltpu.VMEM((2 * rows, depth), jnp.bfloat16)],
        name="products",
        mib=16,
        flops=flops,
    )(*blocks, basis)


def sum_kernel(*refs):
    *arrived, out = refs
    at = 0
    for ref in arrived:
        total = ref[0]
        for k in range(1, ref.shape[0]):
            total = total + ref[k]
        rows = total.shape[0]
        for k in range(out.shape[0]):
            out[k, at : at + rows, :] = total
        at += rows


def sum_copies(*arrived, copies=8):
    cols = arrived[0].shape[2]
    rows = sum(part.shape[1] for part in arrived)
    return call(sum_kernel, f32(copies, rows, cols), [VMEM] * len(arrived), name="sum_copies")(*arrived)


def in_pieces(value, n):
    return value.reshape(n, -1, value.shape[1])


def grads_kernel(place, grads, basis, own, other):
    rows = own.shape[0]
    basis_high, basis_low = halved(basis[...])

    def product(a, b):
        return lax.dot_general(
            a, b, (((0,), (0,)), ((), ())), preferred_element_type=jnp.float32
        )

    for out, half in ((other, 1 - place[1]), (own, place[1])):
        high, low = halved(grads[:, pl.ds(pl.multiple_of(half * rows, rows), rows)])
        out[...] = product(high, basis_high) + (
            product(low, basis_high) + product(high, basis_low)
        )


def halves_kernel(place, own, arrived, keep, send):
    rows = keep.shape[0]
    kept = pl.ds(pl.multiple_of(place[2] * rows, rows), rows)
    sent = pl.ds(pl.multiple_of((1 - place[2]) * rows, rows), rows)
    keep[...] = own[kept, :] + arrived[kept, :]
    send[...] = own[sent, :] + arrived[sent, :]


def add_kernel(a, b, out):
    out[...] = a[...] + b[...]


def pair_kernel(place, own, other, out):
    rows = own.shape[1]
    out[pl.ds(pl.multiple_of(place[2] * rows, rows), rows), :] = own[0]
    out[pl.ds(pl.multiple_of((1 - place[2]) * rows, rows), rows), :] = other[0]


def place_kernel(place, *refs):
    *pieces, out = refs
    rows = pieces[0].shape[0] // 2
    for ref, distance in zip(pieces, AROUND):
        row = lax.rem(place[0] + distance + 8, 8) * rows
        for lo in range(2):
            into = pl.ds(pl.multiple_of(lo * 8 * rows + row, rows), rows)
            out[into, :] = ref[lo * rows : (lo + 1) * rows, :]


def split_store(value, high_ref, low_ref, row):
    high = value.astype(jnp.bfloat16)
    rows = pl.ds(pl.multiple_of(row, BLOCK), value.shape[0])
    high_ref[rows, :] = high
    low_ref[rows, :] = (value - high.astype(jnp.float32)).astype(jnp.bfloat16)


def split_grads_kernel(place, own, other, high, low):
    rows = own.shape[0]
    for ref, core in ((own, place[1]), (other, 1 - place[1])):
        into = pl.ds(pl.multiple_of(core * rows, rows), rows)
        high[into, :], low[into, :] = halved(ref[...])
    for ref in (high, low):
        ref[2 * rows :, :] = jnp.zeros((DEPTH, own.shape[1]), jnp.bfloat16)


def moments_kernel(place, bounds, *refs):
    acts_refs, (grads_high, grads_low, out) = refs[:2], refs[2:5]
    acts_high, acts_low, moment = refs[5:]
    z, core, lo = place[0], place[1], place[2]
    cols = out.shape[0]
    first_rows = 2 * len(FIRST) * BLOCK // 8
    for from_other in range(2):
        of_core = 1 - core if from_other else core
        ref = acts_refs[from_other]
        sides = slice(cols, 2 * cols) if from_other else slice(0, cols)
        blocks = [(distance, far) for distance in FIRST for far in range(2)]
        rest = [(distance, far) for distance in (*SECOND, LAST) for far in range(2)]
        for start, size, listed in ((0, first_rows, blocks), (first_rows, 64 - first_rows, rest)):
            for at, (distance, far) in enumerate(listed):
                parts, row = [], at * BLOCK
                while row < (at + 1) * BLOCK:
                    inner = row % size
                    count = min(size - inner, (at + 1) * BLOCK - row)
                    spot = start + inner
                    parts.append(ref[row // size, spot : spot + count, sides])
                    row += count
                value = parts[0] if len(parts) == 1 else jnp.concatenate(parts, 0)
                xl = 1 - lo if far else lo
                row = ((xl * 8 + lax.rem(z + distance + 8, 8)) * 2 + of_core) * BLOCK
                split_store(value, acts_high, acts_low, row)
    for ref in (acts_high, acts_low):
        ref[TOKENS:, :] = jnp.zeros((DEPTH, cols), jnp.bfloat16)

    def product(a, b):
        return lax.dot_general(
            a, b, (((0,), (0,)), ((), ())), preferred_element_type=jnp.float32
        )

    out[...] = jnp.zeros_like(out)

    def add_sequence(seq, carry):
        first, end = bounds[seq], bounds[seq + 1]
        base = (first // 16) * 16

        def block(step):
            start = pl.multiple_of(base + step * DEPTH, 16)
            rows = pl.ds(start, DEPTH)
            number = start + lax.broadcasted_iota(jnp.int32, (DEPTH, 1), 0)
            mine = (number >= first) & (number < end)
            grads_h, grads_l = [
                jnp.where(mine, ref[rows, :].astype(jnp.float32), 0.0).astype(jnp.bfloat16)
                for ref in (grads_high, grads_low)
            ]
            acts_h, acts_l = acts_high[rows, :], acts_low[rows, :]
            return product(acts_h, grads_h) + (
                product(acts_l, grads_h) + product(acts_h, grads_l)
            )

        moment[...] = block(0)

        def add_block(step, carry):
            moment[...] += block(step)
            return carry

        lax.fori_loop(1, (end - base + DEPTH - 1) // DEPTH, add_block, 0)
        out[...] += moment[...] * moment[...] * (1.0 / SEQS)
        return carry

    lax.fori_loop(0, SEQS, add_sequence, 0)


def eigenvalues(place, acts, grads, seq_ids):
    labels = jnp.arange(SEQS + 1, dtype=jnp.int32)
    bounds = jnp.sum((seq_ids[None, :] < labels[:, None]).astype(jnp.int32), axis=1)
    cols, out_cols = acts[0].shape[2] // 2, grads[0].shape[1]
    grads = call(
        split_grads_kernel,
        [bf16(TOKENS + DEPTH, out_cols)] * 2,
        [SMEM, VMEM, VMEM],
        name="split_grads",
    )(place, *grads)
    return call(
        moments_kernel,
        f32(cols, out_cols),
        [SMEM, SMEM] + [VMEM] * (len(acts) + len(grads)),
        [
            pltpu.VMEM((TOKENS + DEPTH, cols), jnp.bfloat16),
            pltpu.VMEM((TOKENS + DEPTH, cols), jnp.bfloat16),
            pltpu.VMEM((cols, out_cols), jnp.float32),
        ],
        name="moments",
        mib=28,
    )(place, bounds, *acts, *grads)


def tied(values, *others):
    held = lax.optimization_barrier((tuple(values), others))
    return list(held[0])


def per_device(activations, act_basis, grads, grad_basis, seq_ids):
    place = jnp.stack([lax.axis_index("z"), lax.axis_index("c"), lax.axis_index("xl")])
    place = place.astype(jnp.int32)
    half, cols = grads.shape[0] // 2, grad_basis.shape[1]

    def placed(kernel, shapes, name, *values):
        specs = [SMEM] + [VMEM] * len(values)
        return call(kernel, shapes, specs, name=name)(place, *values)

    other_basis = shifted(act_basis, "c").T
    arrived = shifted(activations, "xl")
    own, other = placed(
        grads_kernel, [f32(half, cols)] * 2, "rotate_grads", grads.T, grad_basis
    )
    arrived, own, other = tied([arrived, own, other])
    block = jnp.concatenate([activations, arrived], 0)
    keep, send = placed(
        halves_kernel, [f32(half // 2, cols)] * 2, "add_halves", own, shifted(other, "c")
    )

    near = [shifted(block, "z", 1), shifted(block, "z", -1)]
    part = call(add_kernel, f32(half // 2, cols), [VMEM, VMEM], name="add")(
        keep, shifted(send, "xl")
    )
    part_arrived = swapped(in_pieces(part, 8), "z")
    second = [shifted(near[0], "z", 1), shifted(near[1], "z", -1)]
    basis = split_basis(*tied([act_basis.T, other_basis], near[0]))
    *second, basis = tied([*second, basis])
    third = [shifted(second[0], "z", 1), shifted(second[1], "z", -1)]
    first_products = products([block, *near, *second], basis, 1000)
    first_products, part_arrived = tied([first_products, part_arrived])
    first_arrived = swapped(in_pieces(first_products, 8), NARROW)

    far = [shifted(third[0][:BLOCK], "z", 1), shifted(third[1][BLOCK:], "z", -1)]
    basis = split_basis(*tied([act_basis.T, other_basis], third[0]))
    *far, basis = tied([*far, basis])
    second_products = products([*third, *far], basis, 5 * 10**9)
    piece = sum_copies(part_arrived, copies=1)
    far_piece, second_products = tied([shifted(piece, "xl"), second_products])
    part = placed(pair_kernel, f32(2 * piece.shape[1], cols), "pair", piece, far_piece)
    second_products, first_arrived, part = tied([second_products, first_arrived, part])
    second_arrived = swapped(in_pieces(second_products, 8), NARROW)

    up1, down1 = shifted(part, "z", 1), shifted(part, "z", -1)
    second_arrived, up1, down1 = tied([second_arrived, up1, down1])
    acts = swapped(sum_copies(first_arrived, second_arrived), NARROW)
    up2, down2 = shifted(up1, "z", 1), shifted(down1, "z", -1)
    up3, down3 = shifted(up2, "z", 1), shifted(down2, "z", -1)
    parts = [part, up1, down1, up2, down2, up3, down3, shifted(up3, "z", 1)]
    part = placed(place_kernel, f32(half, cols), "place", *parts)
    acts, *parts = tied([acts, part, shifted(part, "c")])
    return eigenvalues(place, [acts, shifted(acts, "c")], parts, seq_ids)


def solution(mesh):
    split = Mesh(mesh.devices.reshape(tuple(SIZES.values())), tuple(SIZES))
    return jax.shard_map(
        per_device,
        mesh=split,
        in_specs=(P(WIDE, NARROW), P(NARROW, WIDE), P(None, WIDE), P(WIDE, NARROW), P()),
        out_specs=P(WIDE, NARROW),
        check_vma=False,
    )
```

```python
import functools

import jax
import jax.numpy as jnp
from jax import lax
from jax.experimental import pallas as pl
from jax.experimental.pallas import tpu as pltpu
from jax.sharding import Mesh
from jax.sharding import PartitionSpec as P

SEQS = 4
SIZES = {"xl": 2, "z": 8, "c": 2, "xh": 2, "y": 4}
WIDE = ("xl", "z", "c")
NARROW = ("xh", "y")
TOKENS = 1024
BLOCK = 32
DEPTH = 256
FIRST, SECOND, LAST = (0, -1, 1, -2, 2), (-3, 3), 4
AROUND = (0, -1, 1, -2, 2, -3, 3, 4)
VMEM = pl.BlockSpec(memory_space=pltpu.VMEM)
SMEM = pl.BlockSpec(memory_space=pltpu.SMEM)


def shifted(value, axis, by=1):
    n = SIZES[axis]
    return lax.ppermute(value, axis, [(i, (i + by) % n) for i in range(n)])


def after(value, other):
    return lax.optimization_barrier((value, other))[0]


def swapped(value, axes):
    return lax.all_to_all(value, axes, 0, 0)


def halved(value):
    high = value.astype(jnp.bfloat16)
    return high, (value - high.astype(jnp.float32)).astype(jnp.bfloat16)


def call(kernel, shapes, in_specs, scratch=(), name=None, mib=12, flops=1000):
    return pl.pallas_call(
        kernel,
        out_shape=shapes,
        in_specs=in_specs,
        out_specs=VMEM if not isinstance(shapes, list) else [VMEM] * len(shapes),
        scratch_shapes=list(scratch),
        compiler_params=pltpu.CompilerParams(vmem_limit_bytes=mib << 20),
        cost_estimate=pl.CostEstimate(flops=flops, bytes_accessed=1000, transcendentals=0),
        name=name,
    )


def f32(*shape):
    return jax.ShapeDtypeStruct(shape, jnp.float32)


def bf16(*shape):
    return jax.ShapeDtypeStruct(shape, jnp.bfloat16)


def basis_kernel(own, other, out):
    rows = own.shape[0]
    half = out.shape[1] // 2
    for base, ref in ((0, own), (half, other)):
        start = pl.multiple_of(base + pl.program_id(0) * rows, 16)
        into = pl.ds(start, rows)
        out[0, into, :], out[1, into, :] = halved(ref[...])


def split_basis(own, other):
    rows, depth = own.shape
    block = pl.BlockSpec((rows // 2, depth), lambda step: (step, 0))
    return pl.pallas_call(
        basis_kernel,
        grid=(2,),
        out_shape=pltpu.VMEM((2, 2 * rows, depth), jnp.bfloat16),
        in_specs=[block, block],
        out_specs=VMEM,
        compiler_params=pltpu.CompilerParams(vmem_limit_bytes=50 << 20),
        cost_estimate=pl.CostEstimate(flops=1000, bytes_accessed=1000, transcendentals=0),
        name="split_basis",
    )(own, other)


def products_kernel(*refs):
    *blocks, basis, out, both = refs
    total = out.shape[0]
    at = 0
    for ref in blocks:
        rows = ref.shape[0]
        both[at : at + rows, :], both[total + at : total + at + rows, :] = halved(ref[...])
        at += rows

    def product(a, b):
        return lax.dot_general(
            a, b, (((1,), (1,)), ((), ())), preferred_element_type=jnp.float32
        )

    main = product(both[...], basis[0])
    out[...] = main[:total] + (main[total:] + product(both[:total, :], basis[1]))


def products(blocks, basis, flops):
    rows = sum(block.shape[0] for block in blocks)
    _, cols, depth = basis.shape
    return call(
        products_kernel,
        f32(rows, cols),
        [VMEM] * (1 + len(blocks)),
        [pltpu.VMEM((2 * rows, depth), jnp.bfloat16)],
        name="products",
        mib=16,
        flops=flops,
    )(*blocks, basis)


def sum_kernel(*refs):
    *arrived, out = refs
    at = 0
    for ref in arrived:
        total = ref[0]
        for k in range(1, ref.shape[0]):
            total = total + ref[k]
        rows = total.shape[0]
        for k in range(out.shape[0]):
            out[k, at : at + rows, :] = total
        at += rows


def sum_copies(*arrived, copies=8):
    cols = arrived[0].shape[2]
    rows = sum(part.shape[1] for part in arrived)
    return call(sum_kernel, f32(copies, rows, cols), [VMEM] * len(arrived), name="sum_copies")(*arrived)


def in_pieces(value, n):
    return value.reshape(n, -1, value.shape[1])


def grads_kernel(place, grads, basis, own, other):
    rows = own.shape[0]
    basis_high, basis_low = halved(basis[...])

    def product(a, b):
        return lax.dot_general(
            a, b, (((0,), (0,)), ((), ())), preferred_element_type=jnp.float32
        )

    for out, half in ((other, 1 - place[1]), (own, place[1])):
        high, low = halved(grads[:, pl.ds(pl.multiple_of(half * rows, rows), rows)])
        out[...] = product(high, basis_high) + (
            product(low, basis_high) + product(high, basis_low)
        )


def halves_kernel(place, own, arrived, keep, send):
    rows = keep.shape[0]
    kept = pl.ds(pl.multiple_of(place[2] * rows, rows), rows)
    sent = pl.ds(pl.multiple_of((1 - place[2]) * rows, rows), rows)
    keep[...] = own[kept, :] + arrived[kept, :]
    send[...] = own[sent, :] + arrived[sent, :]


def add_kernel(a, b, out):
    out[...] = a[...] + b[...]


def pair_kernel(place, own, other, out):
    rows = own.shape[1]
    out[pl.ds(pl.multiple_of(place[2] * rows, rows), rows), :] = own[0]
    out[pl.ds(pl.multiple_of((1 - place[2]) * rows, rows), rows), :] = other[0]


def place_kernel(place, *refs):
    *pieces, out = refs
    rows = pieces[0].shape[0] // 2
    for ref, distance in zip(pieces, AROUND):
        row = lax.rem(place[0] + distance + 8, 8) * rows
        for lo in range(2):
            into = pl.ds(pl.multiple_of(lo * 8 * rows + row, rows), rows)
            out[into, :] = ref[lo * rows : (lo + 1) * rows, :]


def split_store(value, high_ref, low_ref, row):
    high = value.astype(jnp.bfloat16)
    rows = pl.ds(pl.multiple_of(row, BLOCK), value.shape[0])
    high_ref[rows, :] = high
    low_ref[rows, :] = (value - high.astype(jnp.float32)).astype(jnp.bfloat16)


def split_grads_kernel(place, own, other, high, low):
    rows = own.shape[0]
    for ref, core in ((own, place[1]), (other, 1 - place[1])):
        into = pl.ds(pl.multiple_of(core * rows, rows), rows)
        high[into, :], low[into, :] = halved(ref[...])
    for ref in (high, low):
        ref[2 * rows :, :] = jnp.zeros((DEPTH, own.shape[1]), jnp.bfloat16)


def moments_kernel(place, bounds, *refs):
    acts_refs, (grads_high, grads_low, out) = refs[:2], refs[2:5]
    acts_high, acts_low, moment = refs[5:]
    z, core, lo = place[0], place[1], place[2]
    cols = out.shape[0]
    first_rows = 2 * len(FIRST) * BLOCK // 8
    for from_other in range(2):
        of_core = 1 - core if from_other else core
        ref = acts_refs[from_other]
        sides = slice(cols, 2 * cols) if from_other else slice(0, cols)
        blocks = [(distance, far) for distance in FIRST for far in range(2)]
        rest = [(distance, far) for distance in (*SECOND, LAST) for far in range(2)]
        for start, size, listed in ((0, first_rows, blocks), (first_rows, 64 - first_rows, rest)):
            for at, (distance, far) in enumerate(listed):
                parts, row = [], at * BLOCK
                while row < (at + 1) * BLOCK:
                    inner = row % size
                    count = min(size - inner, (at + 1) * BLOCK - row)
                    spot = start + inner
                    parts.append(ref[row // size, spot : spot + count, sides])
                    row += count
                value = parts[0] if len(parts) == 1 else jnp.concatenate(parts, 0)
                xl = 1 - lo if far else lo
                row = ((xl * 8 + lax.rem(z + distance + 8, 8)) * 2 + of_core) * BLOCK
                split_store(value, acts_high, acts_low, row)
    for ref in (acts_high, acts_low):
        ref[TOKENS:, :] = jnp.zeros((DEPTH, cols), jnp.bfloat16)

    def product(a, b):
        return lax.dot_general(
            a, b, (((0,), (0,)), ((), ())), preferred_element_type=jnp.float32
        )

    out[...] = jnp.zeros_like(out)

    def add_sequence(seq, carry):
        first, end = bounds[seq], bounds[seq + 1]
        base = (first // 16) * 16

        def block(step):
            start = pl.multiple_of(base + step * DEPTH, 16)
            rows = pl.ds(start, DEPTH)
            number = start + lax.broadcasted_iota(jnp.int32, (DEPTH, 1), 0)
            mine = (number >= first) & (number < end)
            grads_h, grads_l = [
                jnp.where(mine, ref[rows, :].astype(jnp.float32), 0.0).astype(jnp.bfloat16)
                for ref in (grads_high, grads_low)
            ]
            acts_h, acts_l = acts_high[rows, :], acts_low[rows, :]
            return product(acts_h, grads_h) + (
                product(acts_l, grads_h) + product(acts_h, grads_l)
            )

        moment[...] = block(0)

        def add_block(step, carry):
            moment[...] += block(step)
            return carry

        lax.fori_loop(1, (end - base + DEPTH - 1) // DEPTH, add_block, 0)
        out[...] += moment[...] * moment[...] * (1.0 / SEQS)
        return carry

    lax.fori_loop(0, SEQS, add_sequence, 0)


def eigenvalues(place, acts, grads, seq_ids):
    labels = jnp.arange(SEQS + 1, dtype=jnp.int32)
    bounds = jnp.sum((seq_ids[None, :] < labels[:, None]).astype(jnp.int32), axis=1)
    cols, out_cols = acts[0].shape[2] // 2, grads[0].shape[1]
    grads = call(
        split_grads_kernel,
        [bf16(TOKENS + DEPTH, out_cols)] * 2,
        [SMEM, VMEM, VMEM],
        name="split_grads",
    )(place, *grads)
    return call(
        moments_kernel,
        f32(cols, out_cols),
        [SMEM, SMEM] + [VMEM] * (len(acts) + len(grads)),
        [
            pltpu.VMEM((TOKENS + DEPTH, cols), jnp.bfloat16),
            pltpu.VMEM((TOKENS + DEPTH, cols), jnp.bfloat16),
            pltpu.VMEM((cols, out_cols), jnp.float32),
        ],
        name="moments",
        mib=28,
    )(place, bounds, *acts, *grads)


def tied(values, *others):
    held = lax.optimization_barrier((tuple(values), others))
    return list(held[0])


def per_device(activations, act_basis, grads, grad_basis, seq_ids):
    place = jnp.stack([lax.axis_index("z"), lax.axis_index("c"), lax.axis_index("xl")])
    place = place.astype(jnp.int32)
    half, cols = grads.shape[0] // 2, grad_basis.shape[1]

    def placed(kernel, shapes, name, *values):
        specs = [SMEM] + [VMEM] * len(values)
        return call(kernel, shapes, specs, name=name)(place, *values)

    other_basis = shifted(act_basis, "c").T
    arrived = shifted(activations, "xl")
    own, other = placed(
        grads_kernel, [f32(half, cols)] * 2, "rotate_grads", grads.T, grad_basis
    )
    arrived, own, other = tied([arrived, own, other])
    block = jnp.concatenate([activations, arrived], 0)
    keep, send = placed(
        halves_kernel, [f32(half // 2, cols)] * 2, "add_halves", own, shifted(other, "c")
    )

    near = [shifted(block, "z", 1), shifted(block, "z", -1)]
    part = call(add_kernel, f32(half // 2, cols), [VMEM, VMEM], name="add")(
        keep, shifted(send, "xl")
    )
    part_arrived = swapped(in_pieces(part, 8), "z")
    second = [shifted(near[0], "z", 1), shifted(near[1], "z", -1)]
    basis = split_basis(*tied([act_basis.T, other_basis], near[0]))
    *second, basis = tied([*second, basis])
    third = [shifted(second[0], "z", 1), shifted(second[1], "z", -1)]
    first_products = products([block, *near, *second], basis, 1000)
    first_products, part_arrived = tied([first_products, part_arrived])
    first_arrived = swapped(in_pieces(first_products, 8), NARROW)

    far = [shifted(third[0][:BLOCK], "z", 1), shifted(third[1][BLOCK:], "z", -1)]
    basis = split_basis(*tied([act_basis.T, other_basis], third[0]))
    *far, basis = tied([*far, basis])
    second_products = products([*third, *far], basis, 5 * 10**9)
    piece = sum_copies(part_arrived, copies=1)
    far_piece, second_products = tied([shifted(piece, "xl"), second_products])
    part = placed(pair_kernel, f32(2 * piece.shape[1], cols), "pair", piece, far_piece)
    second_products, first_arrived, part = tied([second_products, first_arrived, part])
    second_arrived = swapped(in_pieces(second_products, 8), NARROW)

    up1, down1 = shifted(part, "z", 1), shifted(part, "z", -1)
    second_arrived, up1, down1 = tied([second_arrived, up1, down1])
    acts = swapped(sum_copies(first_arrived, second_arrived), NARROW)
    up2, down2 = shifted(up1, "z", 1), shifted(down1, "z", -1)
    up3, down3 = shifted(up2, "z", 1), shifted(down2, "z", -1)
    parts = [part, up1, down1, up2, down2, up3, down3, shifted(up3, "z", 1)]
    part = placed(place_kernel, f32(half, cols), "place", *parts)
    acts, *parts = tied([acts, part, shifted(part, "c")])
    return eigenvalues(place, [acts, shifted(acts, "c")], parts, seq_ids)


def solution(mesh):
    split = Mesh(mesh.devices.reshape(tuple(SIZES.values())), tuple(SIZES))
    return jax.shard_map(
        per_device,
        mesh=split,
        in_specs=(P(WIDE, NARROW), P(NARROW, WIDE), P(None, WIDE), P(WIDE, NARROW), P()),
        out_specs=P(WIDE, NARROW),
        check_vma=False,
    )
```

```python
import functools

import jax
import jax.numpy as jnp
from jax import lax
from jax.experimental import pallas as pl
from jax.experimental.pallas import tpu as pltpu
from jax.sharding import Mesh
from jax.sharding import PartitionSpec as P

SEQS = 4
SIZES = {"xl": 2, "z": 8, "c": 2, "xh": 2, "y": 4}
WIDE = ("xl", "z", "c")
NARROW = ("xh", "y")
TOKENS = 1024
BLOCK = 32
DEPTH = 256
FIRST, SECOND, LAST = (0, -1, 1, -2, 2), (-3, 3), 4
AROUND = (0, -1, 1, -2, 2, -3, 3, 4)
VMEM = pl.BlockSpec(memory_space=pltpu.VMEM)
SMEM = pl.BlockSpec(memory_space=pltpu.SMEM)


def shifted(value, axis, by=1):
    n = SIZES[axis]
    return lax.ppermute(value, axis, [(i, (i + by) % n) for i in range(n)])


def after(value, other):
    return lax.optimization_barrier((value, other))[0]


def swapped(value, axes):
    return lax.all_to_all(value, axes, 0, 0)


def halved(value):
    high = value.astype(jnp.bfloat16)
    return high, (value - high.astype(jnp.float32)).astype(jnp.bfloat16)


def call(kernel, shapes, in_specs, scratch=(), name=None, mib=12, flops=1000):
    return pl.pallas_call(
        kernel,
        out_shape=shapes,
        in_specs=in_specs,
        out_specs=VMEM if not isinstance(shapes, list) else [VMEM] * len(shapes),
        scratch_shapes=list(scratch),
        compiler_params=pltpu.CompilerParams(vmem_limit_bytes=mib << 20),
        cost_estimate=pl.CostEstimate(flops=flops, bytes_accessed=1000, transcendentals=0),
        name=name,
    )


def f32(*shape):
    return jax.ShapeDtypeStruct(shape, jnp.float32)


def bf16(*shape):
    return jax.ShapeDtypeStruct(shape, jnp.bfloat16)


def basis_kernel(own, other, out):
    rows = own.shape[0]
    half = out.shape[1] // 2
    for base, ref in ((0, own), (half, other)):
        start = pl.multiple_of(base + pl.program_id(0) * rows, 16)
        into = pl.ds(start, rows)
        out[0, into, :], out[1, into, :] = halved(ref[...])


def split_basis(own, other):
    rows, depth = own.shape
    block = pl.BlockSpec((rows // 2, depth), lambda step: (step, 0))
    return pl.pallas_call(
        basis_kernel,
        grid=(2,),
        out_shape=pltpu.VMEM((2, 2 * rows, depth), jnp.bfloat16),
        in_specs=[block, block],
        out_specs=VMEM,
        compiler_params=pltpu.CompilerParams(vmem_limit_bytes=50 << 20),
        cost_estimate=pl.CostEstimate(flops=1000, bytes_accessed=1000, transcendentals=0),
        name="split_basis",
    )(own, other)


def products_kernel(known, *refs):
    *inputs, basis, out, both = refs
    base = 0
    for ref in inputs[:known]:
        out[base : base + ref.shape[0], :] = ref[...]
        base += ref.shape[0]
    total = out.shape[0] - base
    at = 0
    for ref in inputs[known:]:
        rows = ref.shape[0]
        both[at : at + rows, :], both[total + at : total + at + rows, :] = halved(ref[...])
        at += rows

    def product(a, b):
        return lax.dot_general(
            a, b, (((1,), (1,)), ((), ())), preferred_element_type=jnp.float32
        )

    main = product(both[...], basis[0])
    out[base:, :] = main[:total] + (main[total:] + product(both[:total, :], basis[1]))


def products(blocks, basis, flops, earlier=()):
    rows = sum(block.shape[0] for block in blocks)
    _, cols, depth = basis.shape
    return call(
        functools.partial(products_kernel, len(earlier)),
        f32(rows + sum(value.shape[0] for value in earlier), cols),
        [VMEM] * (1 + len(blocks) + len(earlier)),
        [pltpu.VMEM((2 * rows, depth), jnp.bfloat16)],
        name="products",
        mib=16,
        flops=flops,
    )(*earlier, *blocks, basis)


def sum_kernel(*refs):
    *arrived, out = refs
    at = 0
    for ref in arrived:
        total = ref[0]
        for k in range(1, ref.shape[0]):
            total = total + ref[k]
        rows = total.shape[0]
        for k in range(out.shape[0]):
            out[k, at : at + rows, :] = total
        at += rows


def sum_copies(*arrived, copies=8):
    cols = arrived[0].shape[2]
    rows = sum(part.shape[1] for part in arrived)
    return call(sum_kernel, f32(copies, rows, cols), [VMEM] * len(arrived), name="sum_copies")(*arrived)


def in_pieces(value, n):
    return value.reshape(n, -1, value.shape[1])


def grads_kernel(place, grads, basis, own, other):
    rows = own.shape[0]
    basis_high, basis_low = halved(basis[...])

    def product(a, b):
        return lax.dot_general(
            a, b, (((0,), (0,)), ((), ())), preferred_element_type=jnp.float32
        )

    for out, half in ((other, 1 - place[1]), (own, place[1])):
        high, low = halved(grads[:, pl.ds(pl.multiple_of(half * rows, rows), rows)])
        out[...] = product(high, basis_high) + (
            product(low, basis_high) + product(high, basis_low)
        )


def halves_kernel(place, own, arrived, keep, send):
    rows = keep.shape[0]
    kept = pl.ds(pl.multiple_of(place[2] * rows, rows), rows)
    sent = pl.ds(pl.multiple_of((1 - place[2]) * rows, rows), rows)
    keep[...] = own[kept, :] + arrived[kept, :]
    send[...] = own[sent, :] + arrived[sent, :]


def add_kernel(a, b, out):
    out[...] = a[...] + b[...]


def pair_kernel(place, own, other, out):
    rows = own.shape[1]
    out[pl.ds(pl.multiple_of(place[2] * rows, rows), rows), :] = own[0]
    out[pl.ds(pl.multiple_of((1 - place[2]) * rows, rows), rows), :] = other[0]


def place_kernel(place, *refs):
    *pieces, out = refs
    rows = pieces[0].shape[0] // 2
    for ref, distance in zip(pieces, AROUND):
        row = lax.rem(place[0] + distance + 8, 8) * rows
        for lo in range(2):
            into = pl.ds(pl.multiple_of(lo * 8 * rows + row, rows), rows)
            out[into, :] = ref[lo * rows : (lo + 1) * rows, :]


def split_store(value, high_ref, low_ref, row):
    high = value.astype(jnp.bfloat16)
    rows = pl.ds(pl.multiple_of(row, BLOCK), value.shape[0])
    high_ref[rows, :] = high
    low_ref[rows, :] = (value - high.astype(jnp.float32)).astype(jnp.bfloat16)


def split_grads_kernel(place, own, other, high, low):
    rows = own.shape[0]
    for ref, core in ((own, place[1]), (other, 1 - place[1])):
        into = pl.ds(pl.multiple_of(core * rows, rows), rows)
        high[into, :], low[into, :] = halved(ref[...])
    for ref in (high, low):
        ref[2 * rows :, :] = jnp.zeros((DEPTH, own.shape[1]), jnp.bfloat16)


def moments_kernel(place, bounds, *refs):
    acts_refs, (grads_high, grads_low, out) = refs[:2], refs[2:5]
    acts_high, acts_low, moment = refs[5:]
    z, core, lo = place[0], place[1], place[2]
    cols = out.shape[0]
    first_rows = 2 * len(FIRST) * BLOCK // 8
    for from_other in range(2):
        of_core = 1 - core if from_other else core
        ref = acts_refs[from_other]
        sides = slice(cols, 2 * cols) if from_other else slice(0, cols)
        blocks = [(distance, far) for distance in FIRST for far in range(2)]
        rest = [(distance, far) for distance in (*SECOND, LAST) for far in range(2)]
        for start, size, listed in ((0, first_rows, blocks), (first_rows, 64 - first_rows, rest)):
            for at, (distance, far) in enumerate(listed):
                parts, row = [], at * BLOCK
                while row < (at + 1) * BLOCK:
                    inner = row % size
                    count = min(size - inner, (at + 1) * BLOCK - row)
                    spot = start + inner
                    parts.append(ref[row // size, spot : spot + count, sides])
                    row += count
                value = parts[0] if len(parts) == 1 else jnp.concatenate(parts, 0)
                xl = 1 - lo if far else lo
                row = ((xl * 8 + lax.rem(z + distance + 8, 8)) * 2 + of_core) * BLOCK
                split_store(value, acts_high, acts_low, row)
    for ref in (acts_high, acts_low):
        ref[TOKENS:, :] = jnp.zeros((DEPTH, cols), jnp.bfloat16)

    def product(a, b):
        return lax.dot_general(
            a, b, (((0,), (0,)), ((), ())), preferred_element_type=jnp.float32
        )

    out[...] = jnp.zeros_like(out)

    def add_sequence(seq, carry):
        first, end = bounds[seq], bounds[seq + 1]
        base = (first // 16) * 16

        def block(step):
            start = pl.multiple_of(base + step * DEPTH, 16)
            rows = pl.ds(start, DEPTH)
            number = start + lax.broadcasted_iota(jnp.int32, (DEPTH, 1), 0)
            mine = (number >= first) & (number < end)
            grads_h, grads_l = [
                jnp.where(mine, ref[rows, :].astype(jnp.float32), 0.0).astype(jnp.bfloat16)
                for ref in (grads_high, grads_low)
            ]
            acts_h, acts_l = acts_high[rows, :], acts_low[rows, :]
            return product(acts_h, grads_h) + (
                product(acts_l, grads_h) + product(acts_h, grads_l)
            )

        moment[...] = block(0)

        def add_block(step, carry):
            moment[...] += block(step)
            return carry

        lax.fori_loop(1, (end - base + DEPTH - 1) // DEPTH, add_block, 0)
        out[...] += moment[...] * moment[...] * (1.0 / SEQS)
        return carry

    lax.fori_loop(0, SEQS, add_sequence, 0)


def eigenvalues(place, acts, grads, seq_ids):
    labels = jnp.arange(SEQS + 1, dtype=jnp.int32)
    bounds = jnp.sum((seq_ids[None, :] < labels[:, None]).astype(jnp.int32), axis=1)
    cols, out_cols = acts[0].shape[2] // 2, grads[0].shape[1]
    grads = call(
        split_grads_kernel,
        [bf16(TOKENS + DEPTH, out_cols)] * 2,
        [SMEM, VMEM, VMEM],
        name="split_grads",
    )(place, *grads)
    return call(
        moments_kernel,
        f32(cols, out_cols),
        [SMEM, SMEM] + [VMEM] * (len(acts) + len(grads)),
        [
            pltpu.VMEM((TOKENS + DEPTH, cols), jnp.bfloat16),
            pltpu.VMEM((TOKENS + DEPTH, cols), jnp.bfloat16),
            pltpu.VMEM((cols, out_cols), jnp.float32),
        ],
        name="moments",
        mib=28,
    )(place, bounds, *acts, *grads)


def tied(values, *others):
    held = lax.optimization_barrier((tuple(values), others))
    return list(held[0])


def per_device(activations, act_basis, grads, grad_basis, seq_ids):
    place = jnp.stack([lax.axis_index("z"), lax.axis_index("c"), lax.axis_index("xl")])
    place = place.astype(jnp.int32)
    half, cols = grads.shape[0] // 2, grad_basis.shape[1]

    def placed(kernel, shapes, name, *values):
        specs = [SMEM] + [VMEM] * len(values)
        return call(kernel, shapes, specs, name=name)(place, *values)

    other_basis = shifted(act_basis, "c").T
    arrived = shifted(activations, "xl")
    own, other = placed(
        grads_kernel, [f32(half, cols)] * 2, "rotate_grads", grads.T, grad_basis
    )
    arrived, own, other = tied([arrived, own, other])
    block = jnp.concatenate([activations, arrived], 0)
    keep, send = placed(
        halves_kernel, [f32(half // 2, cols)] * 2, "add_halves", own, shifted(other, "c")
    )

    near = [shifted(block, "z", 1), shifted(block, "z", -1)]
    part = call(add_kernel, f32(half // 2, cols), [VMEM, VMEM], name="add")(
        keep, shifted(send, "xl")
    )
    part_arrived = swapped(in_pieces(part, 8), "z")
    second = [shifted(near[0], "z", 1), shifted(near[1], "z", -1)]
    basis = split_basis(*tied([act_basis.T, other_basis], near[0]))
    near_products = products([block, *near], basis, 1000)
    *second, basis, near_products = tied([*second, basis, near_products])
    third = [shifted(second[0], "z", 1), shifted(second[1], "z", -1)]
    first_products = products(second, basis, 1000, [near_products])
    first_products, part_arrived = tied([first_products, part_arrived])
    first_arrived = swapped(in_pieces(first_products, 8), NARROW)

    far = [shifted(third[0][:BLOCK], "z", 1), shifted(third[1][BLOCK:], "z", -1)]
    basis = split_basis(*tied([act_basis.T, other_basis], third[0]))
    *far, basis = tied([*far, basis])
    second_products = products([*third, *far], basis, 5 * 10**9)
    piece = sum_copies(part_arrived, copies=1)
    far_piece, second_products = tied([shifted(piece, "xl"), second_products])
    part = placed(pair_kernel, f32(2 * piece.shape[1], cols), "pair", piece, far_piece)
    second_products, first_arrived, part = tied([second_products, first_arrived, part])
    second_arrived = swapped(in_pieces(second_products, 8), NARROW)

    up1, down1 = shifted(part, "z", 1), shifted(part, "z", -1)
    second_arrived, up1, down1 = tied([second_arrived, up1, down1])
    acts = swapped(sum_copies(first_arrived, second_arrived), NARROW)
    up2, down2 = shifted(up1, "z", 1), shifted(down1, "z", -1)
    up3, down3 = shifted(up2, "z", 1), shifted(down2, "z", -1)
    parts = [part, up1, down1, up2, down2, up3, down3, shifted(up3, "z", 1)]
    part = placed(place_kernel, f32(half, cols), "place", *parts)
    acts, *parts = tied([acts, part, shifted(part, "c")])
    return eigenvalues(place, [acts, shifted(acts, "c")], parts, seq_ids)


def solution(mesh):
    split = Mesh(mesh.devices.reshape(tuple(SIZES.values())), tuple(SIZES))
    return jax.shard_map(
        per_device,
        mesh=split,
        in_specs=(P(WIDE, NARROW), P(NARROW, WIDE), P(None, WIDE), P(WIDE, NARROW), P()),
        out_specs=P(WIDE, NARROW),
        check_vma=False,
    )
```
